32 devices in a mesh: energy: 2 (over core), space: 16 (over z, y, x).
Axes of the slice: x: 2, y: 2, z: 4, core: 2. Of those that a mesh axis runs over, the one named last changes fastest.
Arguments:
- precond: bfloat16 [2, 32, 2, 512, 512], P('energy', 'space'), may hold values from -2 to 2
- coupling: bfloat16 [32, 2, 512, 512], P('space'), may hold values from -0.046875 to 0.046875
- source: float32 [2, 32, 2, 512, 128], P('energy', 'space'), may hold values from -6 to 6
- sigma_ret: float32 [2, 32, 2, 512], P('energy', 'space'), may hold values from -0.4 to 0.4
- occupation: float32 [2, 128], replicated, may hold values from 0.05 to 0.95
- shift_offsets: int32 [2, 4], replicated, may hold values from -1 to 1, as said below
- shift_weights: float32 [2, 4], replicated, may hold values from 0.3 to 3
Outputs:
- sigma_lesser: bfloat16 [2, 32, 2, 512, 512], P('energy', 'space')
- sigma_greater: bfloat16 [2, 32, 2, 512, 512], P('energy', 'space')
The draws below stay inside these ranges and needn't reach their ends.
Inputs may be any that keep to these rules, and one draw needn't show every extreme that they name: `shift_offsets`: in every energy's list one offset is -1 or 1.
All inputs are finite; a program needn't handle non-finite values.
Results may differ from the reference program's by a relative error of at most 0.015.
Values may be sent and summed in bfloat16 or wider, within the bound.
No kernel may reach another device: no remote copies, remote signals or barrier semaphores. Data moves between devices by JAX's collectives and lax.ppermute only.
A program may use at most 64 MiB of HBM per device.

```python
import math
import jax
import jax.numpy as jnp
from jax import lax

M = 512
MODES = 128
NSHIFT = 4
SWEEPS = 4
SPAN = 1
NE = 2
NSLAB = 32


def draw_precond(key, part):
    key_noise, key_real, key_imag = jax.random.split(key, 3)
    full_shape = (NE, NSLAB, 2, M, M)
    spread_noise = jax.random.normal(key_noise, full_shape, jnp.float32)
    spread_noise = spread_noise * (0.25 / math.sqrt(M))
    identity = (jnp.arange(M)[:, None] == jnp.arange(M)[None, :]).astype(jnp.float32)
    diagonal_real = jax.random.uniform(key_real, (NE, NSLAB, 1, M, 1), jnp.float32, 0.6, 1.0)
    diagonal_imag = jax.random.uniform(key_imag, (NE, NSLAB, 1, M, 1), jnp.float32, -0.3, -0.05)
    diagonal = jnp.concatenate([diagonal_real, diagonal_imag], axis=2)
    return (spread_noise * (1.0 - identity) + diagonal * identity).astype(jnp.bfloat16)


def draw_shift_offsets(key, part):
    key_offsets, key_sign = jax.random.split(jax.random.fold_in(key, 17))
    drawn = jax.random.randint(key_offsets, (NE, NSHIFT), -SPAN, SPAN + 1, dtype=jnp.int32)
    side_sign = jax.random.randint(key_sign, (NE, 1), 0, 2, dtype=jnp.int32) * 2 - 1
    return jnp.concatenate([side_sign * SPAN, drawn[:, 1:]], axis=1).astype(jnp.int32)


def block_scale(stream_key, extent, pieces, smallest, high):
    gain, own = 1.0, jax.random.fold_in(stream_key, 6)
    for axis_at, parts in pieces:
        draws = jnp.exp(jax.random.uniform(jax.random.fold_in(own, axis_at), (parts,), jnp.float32, smallest / len(pieces), high / len(pieces)))
        gain = gain * jnp.repeat(draws, extent[axis_at] // parts).reshape([-1 if axis == axis_at else 1 for axis in range(len(extent))])
    return gain


def normal_values(rng, shape, width, reach, shards=(), kind=jnp.bfloat16):
    array = width * jax.random.normal(rng, shape, jnp.float32)
    if shards:
        array = array * block_scale(rng, shape, shards, -0.22, 0.18)
    return jnp.clip(array, -reach, reach).astype(kind)


def setup_inputs(seed: int = 0) -> dict:
    splits = jax.random.split(jax.random.key(seed), 8)
    return {
        "precond": draw_precond(jax.random.fold_in(splits[7], 71), 0),
        "coupling": normal_values(splits[1], (NSLAB, 2, M, M), (32 * M) ** -0.5, 0.046875, ((0, 16),)),
        "source": normal_values(splits[2], (NE, NSLAB, 2, M, MODES), 1.0, 6.0, ((0, 2), (1, 16)), jnp.float32),
        "sigma_ret": jnp.clip(jax.random.uniform(splits[3], (NE, NSLAB, 2, M), jnp.float32, -0.4, 0.4) * block_scale(splits[3], (NE, NSLAB, 2, M), ((0, 2), (1, 16)), -0.4, 0.0), -0.4, 0.4),
        "occupation": jnp.clip(jax.random.uniform(splits[4], (NE, MODES), jnp.float32, 0.05, 0.95), 0.05, 0.95),
        "shift_offsets": draw_shift_offsets(jax.random.fold_in(splits[7], 71), 0),
        "shift_weights": jnp.clip(jnp.exp(jax.random.uniform(splits[6], (NE, NSHIFT), jnp.float32, math.log(0.3), math.log(3.0))), 0.3, 3.0),
    }


def round_trip(values):
    return lax.optimization_barrier(values.astype(jnp.bfloat16)).astype(jnp.float32)


def multiply(first_operand, second_operand):
    return jnp.einsum("...mn,...nk->...mk", first_operand.astype(jnp.float32), second_operand.astype(jnp.float32))


def multiply_adjoint(first_operand, second_operand):
    return jnp.einsum("...nm,...nk->...mk", first_operand.astype(jnp.float32), second_operand.astype(jnp.float32))


def complex_product(matrix, states):
    real_part = multiply(matrix[..., 0, :, :], states[..., 0, :, :]) - multiply(matrix[..., 1, :, :], states[..., 1, :, :])
    imag_part = multiply(matrix[..., 0, :, :], states[..., 1, :, :]) + multiply(matrix[..., 1, :, :], states[..., 0, :, :])
    return jnp.stack([real_part, imag_part], axis=-3)


def adjoint_product(matrix, states):
    real_part = multiply_adjoint(matrix[..., 0, :, :], states[..., 0, :, :]) + multiply_adjoint(matrix[..., 1, :, :], states[..., 1, :, :])
    imag_part = multiply_adjoint(matrix[..., 0, :, :], states[..., 1, :, :]) - multiply_adjoint(matrix[..., 1, :, :], states[..., 0, :, :])
    return jnp.stack([real_part, imag_part], axis=-3)


def solve_energy(precond_one, source_one, sigma_one, coupling):
    states = round_trip(complex_product(precond_one, round_trip(source_one)))
    sigma_real = sigma_one[:, 0, :, None]
    sigma_imag = sigma_one[:, 1, :, None]
    for sweep_index in range(1, SWEEPS):
        upper_term = complex_product(coupling[:-1], states[1:])
        upper_term = jnp.concatenate([upper_term, jnp.zeros_like(upper_term[:1])], axis=0)
        lower_term = round_trip(adjoint_product(coupling[:-1], states[:-1]))
        lower_term = jnp.concatenate([jnp.zeros_like(lower_term[:1]), lower_term], axis=0)
        local_real = sigma_real * states[:, 0] - sigma_imag * states[:, 1]
        local_imag = sigma_real * states[:, 1] + sigma_imag * states[:, 0]
        local_term = jnp.stack([local_real, local_imag], axis=1)
        driven = round_trip(source_one + local_term + upper_term + lower_term)
        states = round_trip(complex_product(precond_one, driven))
    return states.astype(jnp.bfloat16)


def reference(precond, coupling, source, sigma_ret, occupation, shift_offsets, shift_weights):
    all_states = lax.map(lambda packed: solve_energy(packed[0], packed[1], packed[2], coupling), (precond, source, sigma_ret))

    def self_energy(energy_index):
        targets = energy_index + shift_offsets[energy_index]
        inside = (targets >= 0) & (targets < NE)
        clipped = jnp.clip(targets, 0, NE - 1).astype(jnp.int32)
        picked = all_states[clipped].astype(jnp.float32)
        occupied = occupation[clipped]
        weights = jnp.where(inside, shift_weights[energy_index], jnp.zeros_like(shift_weights[energy_index])) / MODES

        def block(scale):
            scaled = round_trip(picked * scale[:, None, None, None, :])
            real_part = jnp.einsum("jsmk,jsnk->smn", picked[:, :, 0], scaled[:, :, 0]) + jnp.einsum("jsmk,jsnk->smn", picked[:, :, 1], scaled[:, :, 1])
            imag_part = jnp.einsum("jsmk,jsnk->smn", picked[:, :, 1], scaled[:, :, 0]) - jnp.einsum("jsmk,jsnk->smn", picked[:, :, 0], scaled[:, :, 1])
            return jnp.stack([real_part, imag_part], axis=1).astype(jnp.bfloat16)

        return block(weights[:, None] * occupied), block(weights[:, None] * (1.0 - occupied))

    sigma_lesser, sigma_greater = lax.map(self_energy, jnp.arange(NE, dtype=jnp.int32))
    return (sigma_lesser, sigma_greater)
```

```python
import functools

import jax
import jax.numpy as jnp
from jax import lax
from jax.experimental import pallas as pl
from jax.experimental.pallas import tpu as pltpu
from jax.sharding import PartitionSpec as P

SWEEPS = 4
F32 = jnp.float32
BF16 = jnp.bfloat16
AXES = ("energy", "space")


def times_i(pair, sign):
    half = pair.shape[1] // 2
    real, imag = pair[:, :half], pair[:, half:]
    if sign > 0:
        return jnp.concatenate([-imag, real], axis=1)
    return jnp.concatenate([imag, -real], axis=1)


def product(matrix, pair):
    out = jnp.dot(matrix[0], pair, preferred_element_type=F32)
    return out + jnp.dot(matrix[1], times_i(pair, 1), preferred_element_type=F32)


def transposed_dot(matrix, pair):
    return lax.dot_general(matrix, pair, (((0,), (0,)), ((), ())), preferred_element_type=F32)


def adjoint(matrix, pair):
    out = transposed_dot(matrix[0], pair)
    return out + transposed_dot(matrix[1], times_i(pair, -1))


def joined(ref, slab):
    return jnp.concatenate([ref[slab, 0], ref[slab, 1]], axis=1)


def first_kernel(side, where, precond, coupling, source, states, send):
    odd = where[0]
    slab = odd if side else 1 - odd
    right = slab == 1
    fresh = product(precond.at[slab], joined(source, slab).astype(BF16)).astype(BF16)
    states[...] = fresh

    @pl.when(right)
    def _():
        send[...] = adjoint(coupling.at[1], fresh).astype(BF16)

    @pl.when(jnp.logical_not(right))
    def _():
        send[...] = fresh


def base_kernel(where, coupling, source, sigma, states_a, states_b, base_a, base_b):
    def local(slab, states):
        rows = states.shape[0]
        padded = jnp.concatenate([sigma[slab], jnp.zeros((6, rows), F32)], axis=0)
        columns = jnp.transpose(padded)
        real, imag = columns[:, 0:1], columns[:, 1:2]
        wide = states.astype(F32)
        half = wide.shape[1] // 2
        turned = jnp.concatenate([-wide[:, half:], wide[:, :half]], axis=1)
        return joined(source, slab) + (real * wide + imag * turned)

    def both(states_left, states_right, base_left, base_right):
        left, right = states_left[...], states_right[...]
        base_left[...] = local(0, left) + product(coupling.at[0], right)
        handed = adjoint(coupling.at[0], left).astype(BF16).astype(F32)
        base_right[...] = local(1, right) + handed

    @pl.when(where[0] == 0)
    def _():
        both(states_b, states_a, base_b, base_a)

    @pl.when(where[0] != 0)
    def _():
        both(states_a, states_b, base_a, base_b)


def step_kernel(side, last, where, precond, coupling, base, arrived, states, *rest):
    odd, inner = where[0], where[1]
    slab = odd if side else 1 - odd
    right = slab == 1

    @pl.when(right)
    def _():
        message = arrived[...]
        if side:
            message = jnp.where(inner != 0, message, jnp.zeros_like(message))
        driven = (base[...] + product(coupling.at[1], message)).astype(BF16)
        fresh = product(precond.at[1], driven).astype(BF16)
        states[...] = fresh
        if not last:
            rest[0][...] = adjoint(coupling.at[1], fresh).astype(BF16)

    @pl.when(jnp.logical_not(right))
    def _():
        message = arrived[...]
        if side:
            message = jnp.where(inner != 0, message, jnp.zeros_like(message))
        driven = (base[...] + message.astype(F32)).astype(BF16)
        fresh = product(precond.at[0], driven).astype(BF16)
        states[...] = fresh
        if not last:
            rest[0][...] = fresh


def sigma_kernel(step_rows, where, own, other, scales, *rest):
    lesser, greater, scaled = rest[-3:]
    step = pl.program_id(0)

    @pl.when(step == 0)
    def _():
        for at, states in ((0, own), (1, other)):
            wide = states[...].astype(F32)
            for kind in range(2):
                scaled[2 * at + kind] = (wide * scales[2 * at + kind][None, :]).astype(BF16)

    rows = pl.ds(pl.multiple_of(step * step_rows, step_rows), step_rows)
    contract = (((1,), (1,)), ((), ()))
    for kind, out in ((0, lesser), (1, greater)):
        real, imag = None, None
        for at, states in ((0, own), (1, other)):
            pair = states[rows, :]
            weighted = scaled[2 * at + kind]
            real_part = lax.dot_general(pair, weighted, contract, preferred_element_type=F32)
            imag_part = lax.dot_general(
                times_i(pair, -1), weighted, contract, preferred_element_type=F32
            )
            real = real_part if real is None else real + real_part
            imag = imag_part if imag is None else imag + imag_part
        out[0] = real.astype(BF16)
        out[1] = imag.astype(BF16)


def whole(count):
    return [pl.BlockSpec(memory_space=pltpu.VMEM)] * count


SCALAR = pl.BlockSpec(memory_space=pltpu.SMEM)


def call(kernel, outs, flops, read, *args):
    return pl.pallas_call(
        kernel,
        out_shape=outs,
        in_specs=[SCALAR] + whole(len(args) - 1),
        out_specs=whole(len(outs)),
        compiler_params=pltpu.CompilerParams(vmem_limit_bytes=24 * 2**20),
        cost_estimate=pl.CostEstimate(flops=flops, bytes_accessed=read, transcendentals=0),
    )(*args)


def self_blocks(where, own, other, scales, blocks, previous):
    rows, width = own.shape
    step_rows = rows // 2
    spec = pl.BlockSpec((None, 2, step_rows, rows), lambda step, at: (at[0], 0, step, 0))
    held = pl.BlockSpec((rows, width), lambda step, at: (0, 0))
    aliases = {} if previous is None else {4: 0, 5: 1}
    kept = [] if previous is None else [pl.BlockSpec(memory_space=pl.ANY)] * 2
    return pl.pallas_call(
        functools.partial(sigma_kernel, step_rows),
        out_shape=[jax.ShapeDtypeStruct(blocks, BF16)] * 2,
        grid_spec=pltpu.PrefetchScalarGridSpec(
            num_scalar_prefetch=1,
            grid=(rows // step_rows,),
            in_specs=[held, held, pl.BlockSpec(scales.shape, lambda step, at: (0, 0))] + kept,
            out_specs=[spec, spec],
            scratch_shapes=[pltpu.VMEM((4, rows, width), BF16)],
        ),
        input_output_aliases=aliases,
        compiler_params=pltpu.CompilerParams(vmem_limit_bytes=24 * 2**20),
        cost_estimate=pl.CostEstimate(
            flops=16 * rows * rows * width, bytes_accessed=8 * rows * rows, transcendentals=0
        ),
    )(where, own, other, scales, *([] if previous is None else previous))


def body(energies, chips, precond, coupling, source, sigma_ret, occupation, shift_offsets, shift_weights):
    _, slabs, _, rows, modes = source.shape
    width = 2 * modes
    energy, chip = lax.axis_index("energy"), lax.axis_index("space")
    odd = lax.rem(chip, 2)
    inner = jnp.logical_and(chip > 0, chip < chips - 1).astype(jnp.int32)
    where = jnp.stack([odd, inner]).astype(jnp.int32)

    def at(e, c):
        return e * chips + c

    pairing_a, pairing_b = [], []
    for e in range(energies):
        for c in range(chips):
            pairing_a.append((at(e, c), at(e, c ^ 1)))
            if 0 < c < chips - 1:
                pairing_b.append((at(e, c), at(e, ((c + 1) ^ 1) - 1)))
            else:
                pairing_b.append((at(e, c), at(e ^ 1, c)))
    swap = [(at(e, c), at(e ^ 1, c)) for e in range(energies) for c in range(chips)]

    precond, source, sigma = precond[0], source[0], sigma_ret[0]
    pair = jax.ShapeDtypeStruct((rows, width), BF16)
    total = jax.ShapeDtypeStruct((rows, width), F32)
    one = 4 * rows * rows * width
    big, small = 4 * rows * rows, 2 * rows * width

    states, sends, arrived = [None, None], [None, None], [None, None]
    pairings = (pairing_a, pairing_b)
    for side in range(2):
        states[side], sends[side] = call(
            functools.partial(first_kernel, side),
            [pair, pair],
            2 * one,
            2 * big + 4 * small,
            where,
            precond,
            coupling,
            source,
        )
        arrived[side] = lax.ppermute(sends[side], AXES, pairings[side])
    for sweep in range(1, SWEEPS):
        last = sweep == SWEEPS - 1
        bases = call(
            base_kernel, [total, total], 2 * one, 2 * big + 10 * small, where, coupling, source, sigma, *states
        )
        states = list(states)
        for side in range(2):
            results = call(
                functools.partial(step_kernel, side, last),
                [pair] if last else [pair, pair],
                3 * one,
                2 * big + 5 * small,
                where,
                precond,
                coupling,
                bases[side],
                arrived[side],
            )
            states[side] = results[0]
            if not last:
                arrived[side] = lax.ppermute(results[1], AXES, pairings[side])

    offsets = lax.dynamic_index_in_dim(shift_offsets, energy, 0, keepdims=False)
    weights = lax.dynamic_index_in_dim(shift_weights, energy, 0, keepdims=False) / modes
    scales = []
    for target in (energy, energy ^ 1):
        weight = jnp.sum(jnp.where(energy + offsets == target, weights, jnp.zeros_like(weights)))
        occupied = lax.dynamic_index_in_dim(occupation, target, 0, keepdims=False)
        for filled in (occupied, 1.0 - occupied):
            scales.append(jnp.tile(weight * filled, 2))
    scales = jnp.stack(scales)
    blocks = None
    for side in range(2):
        other = lax.ppermute(states[side], AXES, swap)
        slab = odd if side else 1 - odd
        blocks = self_blocks(
            slab[None].astype(jnp.int32), states[side], other, scales, (slabs, 2, rows, rows), blocks
        )
    return tuple(block[None] for block in blocks)


def solution(mesh):
    energies, chips = mesh.shape["energy"], mesh.shape["space"]
    placed = (
        P("energy", "space", None, None, None),
        P("space", None, None, None),
        P("energy", "space", None, None, None),
        P("energy", "space", None, None),
        P(),
        P(),
        P(),
    )
    return jax.shard_map(
        functools.partial(body, energies, chips),
        mesh=mesh,
        in_specs=placed,
        out_specs=(P("energy", "space", None, None, None), P("energy", "space", None, None, None)),
        check_vma=False,
    )
```

```python
import functools

import jax
import jax.numpy as jnp
from jax import lax
from jax.experimental import pallas as pl
from jax.experimental.pallas import tpu as pltpu
from jax.sharding import PartitionSpec as P

SWEEPS = 4
F32 = jnp.float32
BF16 = jnp.bfloat16
AXES = ("energy", "space")


def times_i(pair, sign):
    half = pair.shape[1] // 2
    real, imag = pair[:, :half], pair[:, half:]
    if sign > 0:
        return jnp.concatenate([-imag, real], axis=1)
    return jnp.concatenate([imag, -real], axis=1)


def product(matrix, pair):
    out = jnp.dot(matrix[0], pair, preferred_element_type=F32)
    return out + jnp.dot(matrix[1], times_i(pair, 1), preferred_element_type=F32)


def transposed_dot(matrix, pair):
    return lax.dot_general(matrix, pair, (((0,), (0,)), ((), ())), preferred_element_type=F32)


def adjoint(matrix, pair):
    out = transposed_dot(matrix[0], pair)
    return out + transposed_dot(matrix[1], times_i(pair, -1))


def joined(ref, slab):
    return jnp.concatenate([ref[slab, 0], ref[slab, 1]], axis=1)


def load(source, held, sem):
    copy = pltpu.make_async_copy(source, held, sem)
    copy.start()
    return copy


def lead_kernel(where, precond, coupling, source, states, send, own, link, drive, sems):
    slab = where[0]
    copies = [
        load(source.at[slab], drive, sems.at[0]),
        load(precond.at[slab, 0], own.at[0], sems.at[1]),
        load(precond.at[slab, 1], own.at[1], sems.at[2]),
        load(coupling.at[1, 0], link.at[0], sems.at[3]),
        load(coupling.at[1, 1], link.at[1], sems.at[4]),
    ]
    copies[0].wait()
    pair = jnp.concatenate([drive[0], drive[1]], axis=1).astype(BF16)
    copies[1].wait()
    partial = jnp.dot(own[0], pair, preferred_element_type=F32)
    copies[2].wait()
    partial = partial + jnp.dot(own[1], times_i(pair, 1), preferred_element_type=F32)
    fresh = partial.astype(BF16)
    states[...] = fresh
    copies[3].wait()
    copies[4].wait()
    send_fresh(slab, link, fresh, send)


def trail_kernel(where, precond, coupling, source, link, states, send, own, inner, drive, sems):
    slab = 1 - where[0]
    copies = [
        load(source.at[slab], drive, sems.at[0]),
        load(precond.at[slab, 0], own.at[0], sems.at[1]),
        load(precond.at[slab, 1], own.at[1], sems.at[2]),
        load(coupling.at[0], inner, sems.at[3]),
    ]
    copies[0].wait()
    pair = jnp.concatenate([drive[0], drive[1]], axis=1).astype(BF16)
    copies[1].wait()
    partial = jnp.dot(own[0], pair, preferred_element_type=F32)
    copies[2].wait()
    partial = partial + jnp.dot(own[1], times_i(pair, 1), preferred_element_type=F32)
    fresh = partial.astype(BF16)
    states[...] = fresh
    send_fresh(slab, link, fresh, send)
    copies[3].wait()


def send_fresh(slab, link, fresh, send):
    @pl.when(slab == 1)
    def _():
        send[...] = adjoint(link, fresh).astype(BF16)

    @pl.when(slab == 0)
    def _():
        send[...] = fresh


def chain_kernel(where, own_a, own_b, link, chain):
    def write(own):
        rows = jnp.concatenate([link[0], link[1]], axis=1)
        both = product(own, rows)
        half = both.shape[1] // 2
        chain[0] = both[:, :half].astype(BF16)
        chain[1] = both[:, half:].astype(BF16)

    @pl.when(where[0] != 0)
    def _():
        write(own_a)

    @pl.when(where[0] == 0)
    def _():
        write(own_b)


def base_kernel(first, where, inner, sigma, own_a, own_b, source_a, source_b, states_a, states_b, *rest):
    base_a, base_b = rest[-2:]
    if first:
        occupation, offsets, weights, scales, base_a, base_b = rest
        write_scales(where[2], occupation, offsets, weights, scales)

    def local(slab, source, states):
        rows = states.shape[0]
        padded = jnp.concatenate([sigma[slab], jnp.zeros((6, rows), F32)], axis=0)
        columns = jnp.transpose(padded)
        real, imag = columns[:, 0:1], columns[:, 1:2]
        wide = states.astype(F32)
        half = wide.shape[1] // 2
        turned = jnp.concatenate([-wide[:, half:], wide[:, :half]], axis=1)
        drive = jnp.concatenate([source[0], source[1]], axis=1)
        return drive + (real * wide + imag * turned)

    def both(own, source_left, source_right, states_left, states_right, base_left, base_right):
        left, right = states_left[...], states_right[...]
        handed = adjoint(inner, left).astype(BF16).astype(F32)
        driven = (local(1, source_right, right) + handed).astype(BF16)
        base_right[...] = product(own, driven)
        base_left[...] = local(0, source_left, left) + product(inner, right)

    @pl.when(where[0] != 0)
    def _():
        both(own_a, source_b, source_a, states_b, states_a, base_b, base_a)

    @pl.when(where[0] == 0)
    def _():
        both(own_b, source_a, source_b, states_a, states_b, base_a, base_b)


def write_scales(energy, occupation, offsets, weights, scales):
    modes = occupation.shape[1]
    rows = []
    for at, target in ((0, energy), (1, 1 - energy)):
        total = jnp.float32(0)
        for shift in range(offsets.shape[1]):
            reached = energy + offsets[energy, shift] == target
            total = total + jnp.where(reached, weights[energy, shift], jnp.float32(0))
        weight = jnp.full((1, modes), total, F32) / modes
        filled = occupation[pl.ds(target, 1), :]
        for kind, share in ((0, filled), (1, 1.0 - filled)):
            row = weight * share
            rows.append(jnp.concatenate([row, row], axis=1))
    rows = jnp.concatenate(rows + [jnp.zeros((8 - len(rows), 2 * modes), F32)], axis=0)
    scales[...] = jnp.transpose(rows)


def step_kernel(side, last, where, own, chain, link, base, arrived, *rest):
    states = rest[-1] if last else rest[-2]
    odd, inner = where[0], where[1]
    slab = 1 - odd if side else odd

    def message():
        if side:
            return arrived[...]
        return jnp.where(inner != 0, arrived[...], jnp.zeros_like(arrived))

    @pl.when(slab == 1)
    def _():
        fresh = (base[...] + product(chain, message())).astype(BF16)
        states[...] = fresh
        if not last:
            rest[-1][...] = adjoint(link, fresh).astype(BF16)

    @pl.when(slab == 0)
    def _():
        driven = (base[...] + message().astype(F32)).astype(BF16)
        fresh = product(own, driven).astype(BF16)
        states[...] = fresh
        if not last:
            rest[-1][...] = fresh


def sigma_kernel(where, own, other, scales, *rest):
    lesser, greater, left, right, held, sems = rest[-6:]
    rows, width = own.shape
    half = rows // 2
    for at, states in ((0, own), (1, other)):
        columns = slice(at * width, (at + 1) * width)
        pair = states[...]
        left[:rows, columns] = pair
        left[rows:, columns] = times_i(pair, -1)
        wide = jnp.transpose(pair).astype(F32)
        for kind in range(2):
            scale = scales[:, 2 * at + kind : 2 * at + kind + 1]
            right[kind, columns, :] = (wide * scale).astype(BF16)
    copies = []
    for kind, out in ((0, lesser), (1, greater)):
        for part in range(2):
            columns = slice(part * half, (part + 1) * half)
            block = jnp.dot(left[...], right[kind, :, columns], preferred_element_type=F32)
            held[kind, part, 0] = block[:rows].astype(BF16)
            held[kind, part, 1] = block[rows:].astype(BF16)
            copies.append(
                load(held.at[kind, part], out.at[where[0], :, :, columns], sems.at[kind, part])
            )
    for copy in copies:
        copy.wait()


def whole(count):
    return [pl.BlockSpec(memory_space=pltpu.VMEM)] * count


SCALAR = pl.BlockSpec(memory_space=pltpu.SMEM)
FAR = pl.BlockSpec(memory_space=pltpu.HBM)
NEAR = pl.BlockSpec(memory_space=pltpu.VMEM)


def call(kernel, outs, specs, args, scratch=()):
    return pl.pallas_call(
        kernel,
        out_shape=outs,
        in_specs=specs,
        out_specs=[NEAR] * len(outs),
        scratch_shapes=list(scratch),
        compiler_params=pltpu.CompilerParams(vmem_limit_bytes=24 * 2**20),
        cost_estimate=pl.CostEstimate(flops=1000, bytes_accessed=1000, transcendentals=0),
    )(*args)


def self_blocks(where, own, other, scales, blocks, after, previous):
    rows, width = own.shape
    extra = [after] if previous is None else previous
    kept = [NEAR] if previous is None else [pl.BlockSpec(memory_space=pl.ANY)] * 2
    return pl.pallas_call(
        sigma_kernel,
        out_shape=[jax.ShapeDtypeStruct(blocks, BF16)] * 2,
        in_specs=[SCALAR, NEAR, NEAR, NEAR] + kept,
        out_specs=[pl.BlockSpec(memory_space=pl.ANY)] * 2,
        scratch_shapes=[
            pltpu.VMEM((2 * rows, 2 * width), BF16),
            pltpu.VMEM((2, 2 * width, rows), BF16),
            pltpu.VMEM((2, 2, 2, rows, rows // 2), BF16),
            pltpu.SemaphoreType.DMA((2, 2)),
        ],
        input_output_aliases={} if previous is None else {4: 0, 5: 1},
        compiler_params=pltpu.CompilerParams(vmem_limit_bytes=24 * 2**20),
        cost_estimate=pl.CostEstimate(flops=1000, bytes_accessed=1000, transcendentals=0),
    )(where, own, other, scales, *extra)


def body(energies, chips, precond, coupling, source, sigma_ret, occupation, shift_offsets, shift_weights):
    _, slabs, _, rows, modes = source.shape
    width = 2 * modes
    energy, chip = lax.axis_index("energy"), lax.axis_index("space")
    odd = lax.rem(chip, 2)
    inner = jnp.logical_and(chip > 0, chip < chips - 1).astype(jnp.int32)
    where = jnp.stack([odd, inner, energy]).astype(jnp.int32)

    def at(e, c):
        return e * chips + c

    pairing_a, pairing_b = [], []
    for e in range(energies):
        for c in range(chips):
            pairing_a.append((at(e, c), at(e, c ^ 1)))
            if 0 < c < chips - 1:
                pairing_b.append((at(e, c), at(e, ((c + 1) ^ 1) - 1)))
            else:
                pairing_b.append((at(e, c), at(e ^ 1, c)))
    swap = [(at(e, c), at(e ^ 1, c)) for e in range(energies) for c in range(chips)]

    precond, source, sigma = precond[0], source[0], sigma_ret[0]
    pair = jax.ShapeDtypeStruct((rows, width), BF16)
    total = jax.ShapeDtypeStruct((rows, width), F32)
    matrix = jax.ShapeDtypeStruct((2, rows, rows), BF16)
    drive = jax.ShapeDtypeStruct((2, rows, modes), F32)
    states, arrived = [None, None], [None, None]
    owns, drives = [None, None], [None, None]

    precond, coupling, source = [
        pltpu.with_memory_space_constraint(array, pltpu.HBM) for array in (precond, coupling, source)
    ]
    states[0], send, owns[0], link, drives[0] = call(
        lead_kernel,
        [pair, pair, matrix, matrix, drive],
        [SCALAR, FAR, FAR, FAR],
        (where, precond, coupling, source),
        [pltpu.SemaphoreType.DMA((5,))],
    )
    arrived[0] = lax.ppermute(send, AXES, pairing_b)
    states[1], send, owns[1], within, drives[1] = call(
        trail_kernel,
        [pair, pair, matrix, matrix, drive],
        [SCALAR, FAR, FAR, FAR, NEAR],
        (where, precond, coupling, source, link),
        [pltpu.SemaphoreType.DMA((4,))],
    )
    arrived[1] = lax.ppermute(send, AXES, pairing_a)
    for sweep in range(1, SWEEPS):
        first, last = sweep == 1, sweep == SWEEPS - 1
        bases = call(
            functools.partial(base_kernel, first),
            [jax.ShapeDtypeStruct((width, 8), F32)] * first + [total, total],
            [SCALAR] + [NEAR] * 8 + [NEAR, SCALAR, SCALAR] * first,
            (where, within, sigma, *owns, *drives, *states) + (occupation, shift_offsets, shift_weights) * first,
        )
        if first:
            scales, bases = bases[0], bases[1:]
            (chain,) = call(
                chain_kernel, [matrix], [SCALAR] + [NEAR] * 3, (where, *owns, link)
            )
        states = list(states)
        for side in range(2):
            results = call(
                functools.partial(step_kernel, side, last),
                [pair] if last else [pair, pair],
                [SCALAR] + [NEAR] * 5,
                (where, owns[side], chain, link, bases[side], arrived[side]),
            )
            states[side] = results[0]
            if not last:
                arrived[side] = lax.ppermute(results[1], AXES, (pairing_b, pairing_a)[side])
    others = [lax.ppermute(states[side], AXES, swap) for side in range(2)]
    blocks = None
    for side in range(2):
        slab = 1 - odd if side else odd
        blocks = self_blocks(
            slab[None].astype(jnp.int32),
            states[side],
            others[side],
            scales,
            (slabs, 2, rows, rows),
            states[1] if blocks is None else None,
            blocks,
        )
    return tuple(block[None] for block in blocks)


def solution(mesh):
    energies, chips = mesh.shape["energy"], mesh.shape["space"]
    placed = (
        P("energy", "space", None, None, None),
        P("space", None, None, None),
        P("energy", "space", None, None, None),
        P("energy", "space", None, None),
        P(),
        P(),
        P(),
    )
    return jax.shard_map(
        functools.partial(body, energies, chips),
        mesh=mesh,
        in_specs=placed,
        out_specs=(P("energy", "space", None, None, None), P("energy", "space", None, None, None)),
        check_vma=False,
    )
```

```python
import functools

import jax
import jax.numpy as jnp
from jax import lax
from jax.experimental import pallas as pl
from jax.experimental.pallas import tpu as pltpu
from jax.sharding import PartitionSpec as P

SWEEPS = 4
F32 = jnp.float32
BF16 = jnp.bfloat16
AXES = ("energy", "space")
LEAD_A = True
LEAD_PIECES = 2
HOLD = True


def times_i(pair, sign):
    half = pair.shape[1] // 2
    real, imag = pair[:, :half], pair[:, half:]
    if sign > 0:
        return jnp.concatenate([-imag, real], axis=1)
    return jnp.concatenate([imag, -real], axis=1)


def product(matrix, pair):
    out = jnp.dot(matrix[0], pair, preferred_element_type=F32)
    return out + jnp.dot(matrix[1], times_i(pair, 1), preferred_element_type=F32)


def transposed_dot(matrix, pair):
    return lax.dot_general(matrix, pair, (((0,), (0,)), ((), ())), preferred_element_type=F32)


def adjoint(matrix, pair):
    out = transposed_dot(matrix[0], pair)
    return out + transposed_dot(matrix[1], times_i(pair, -1))


def joined(ref, slab):
    return jnp.concatenate([ref[slab, 0], ref[slab, 1]], axis=1)


def load(source, held, sem):
    copy = pltpu.make_async_copy(source, held, sem)
    copy.start()
    return copy


def lead_kernel(where, precond, coupling, source, states, send, own, link, drive, sems):
    slab = where[0]
    copies = [
        load(source.at[slab], drive, sems.at[0]),
        load(precond.at[slab, 0], own.at[0], sems.at[1]),
        load(precond.at[slab, 1], own.at[1], sems.at[2]),
        load(coupling.at[1, 0], link.at[0], sems.at[3]),
        load(coupling.at[1, 1], link.at[1], sems.at[4]),
    ]
    copies[0].wait()
    pair = jnp.concatenate([drive[0], drive[1]], axis=1).astype(BF16)
    copies[1].wait()
    partial = jnp.dot(own[0], pair, preferred_element_type=F32)
    copies[2].wait()
    partial = partial + jnp.dot(own[1], times_i(pair, 1), preferred_element_type=F32)
    fresh = partial.astype(BF16)
    states[...] = fresh
    copies[3].wait()
    copies[4].wait()
    send_fresh(slab, link, fresh, send)


def trail_kernel(
    where, precond, coupling, source, link, lead, lead_states,
    states, send, own, inner, drive, chain, term, sems,
):
    slab = 1 - where[0]
    copies = [
        load(source.at[slab], drive, sems.at[0]),
        load(precond.at[slab, 0], own.at[0], sems.at[1]),
        load(precond.at[slab, 1], own.at[1], sems.at[2]),
        load(coupling.at[0], inner, sems.at[3]),
    ]
    copies[0].wait()
    pair = jnp.concatenate([drive[0], drive[1]], axis=1).astype(BF16)
    copies[1].wait()
    partial = jnp.dot(own[0], pair, preferred_element_type=F32)
    copies[2].wait()
    partial = partial + jnp.dot(own[1], times_i(pair, 1), preferred_element_type=F32)
    fresh = partial.astype(BF16)
    states[...] = fresh
    send_fresh(slab, link, fresh, send)

    def write_chain(matrix):
        both = product(matrix, jnp.concatenate([link[0], link[1]], axis=1))
        half = both.shape[1] // 2
        chain[0] = both[:, :half].astype(BF16)
        chain[1] = both[:, half:].astype(BF16)

    @pl.when(slab == 1)
    def _():
        write_chain(own)

    @pl.when(slab == 0)
    def _():
        write_chain(lead)

    copies[3].wait()
    write_term(slab, inner, lead_states, term)


def send_fresh(slab, link, fresh, send):
    @pl.when(slab == 1)
    def _():
        send[...] = adjoint(link, fresh).astype(BF16)

    @pl.when(slab == 0)
    def _():
        send[...] = fresh


def write_term(slab, inner, states, term):
    @pl.when(slab == 0)
    def _():
        term[...] = product(inner, states[...])

    @pl.when(slab == 1)
    def _():
        term[...] = adjoint(inner, states[...]).astype(BF16).astype(F32)


def term_kernel(where, inner, states, term):
    write_term(1 - where[0], inner, states, term)


def base_kernel(kind, where, inner, sigma, own_a, own_b, source_a, source_b, states_a, states_b, term, *rest):
    if kind == "first":
        occupation, offsets, weights, base_a, base_b, scales = rest
        write_scales(where[3], occupation, offsets, weights, scales)
    elif kind == "holding":
        waiting, base_a, base_b, send = rest
        send[...] = waiting[...]
    else:
        base_a, base_b = rest

    def local(slab, source, states):
        rows = states.shape[0]
        padded = jnp.concatenate([sigma[slab], jnp.zeros((6, rows), F32)], axis=0)
        columns = jnp.transpose(padded)
        real, imag = columns[:, 0:1], columns[:, 1:2]
        wide = states[...].astype(F32)
        half = wide.shape[1] // 2
        turned = jnp.concatenate([-wide[:, half:], wide[:, :half]], axis=1)
        drive = jnp.concatenate([source[0], source[1]], axis=1)
        return drive + (real * wide + imag * turned)

    @pl.when(where[0] == 1)
    def _():
        handed = adjoint(inner, states_b[...]).astype(BF16).astype(F32)
        base_a[...] = product(own_a, (local(1, source_a, states_a) + handed).astype(BF16))
        base_b[...] = local(0, source_b, states_b) + term[...]

    @pl.when(where[0] == 0)
    def _():
        base_a[...] = local(0, source_a, states_a) + product(inner, states_b[...])
        driven = (local(1, source_b, states_b) + term[...]).astype(BF16)
        base_b[...] = product(own_b, driven)


def write_scales(energy, occupation, offsets, weights, scales):
    modes = occupation.shape[1]
    rows = []
    for at, target in ((0, energy), (1, 1 - energy)):
        total = jnp.float32(0)
        for shift in range(offsets.shape[1]):
            reached = energy + offsets[energy, shift] == target
            total = total + jnp.where(reached, weights[energy, shift], jnp.float32(0))
        weight = jnp.full((1, modes), total, F32) / modes
        filled = occupation[pl.ds(target, 1), :]
        for kind, share in ((0, filled), (1, 1.0 - filled)):
            row = weight * share
            rows.append(jnp.concatenate([row, row], axis=1))
    rows = jnp.concatenate(rows + [jnp.zeros((8 - len(rows), 2 * modes), F32)], axis=0)
    scales[...] = jnp.transpose(rows)


def step_kernel(side, last, outs, where, own, chain, link, base, arrived, *rest):
    results = rest[len(rest) - outs :]
    slab = 1 - where[0] if side else where[0]

    def message():
        return jnp.where(where[1 + side] != 0, arrived[...], jnp.zeros_like(arrived))

    def keep(fresh):
        if not last:
            results[0][...] = fresh
            return
        rows = fresh.shape[0] // outs
        for at, piece in enumerate(results):
            piece[...] = fresh[at * rows : (at + 1) * rows]

    @pl.when(slab == 1)
    def _():
        fresh = (base[...] + product(chain, message())).astype(BF16)
        keep(fresh)
        if not last:
            results[1][...] = adjoint(link, fresh).astype(BF16)

    @pl.when(slab == 0)
    def _():
        driven = (base[...] + message().astype(F32)).astype(BF16)
        fresh = product(own, driven).astype(BF16)
        keep(fresh)
        if not last:
            results[1][...] = fresh


def weighted_squares(parts, scales, at):
    pair = jnp.concatenate([part[...] for part in parts], axis=0)
    half = pair.shape[0] // 2
    turned = times_i(pair, -1)
    upper = jnp.concatenate([pair[:half], turned[:half]], axis=0)
    lower = jnp.concatenate([pair[half:], turned[half:]], axis=0)
    wide = jnp.transpose(pair).astype(F32)
    for kind in range(2):
        weighted = (wide * scales[:, 2 * at + kind : 2 * at + kind + 1]).astype(BF16)
        yield (
            kind,
            jnp.dot(upper, weighted, preferred_element_type=F32),
            jnp.dot(lower, weighted[:, half:], preferred_element_type=F32),
        )


def own_sigma_kernel(pieces, scales, *rest):
    tops, lows = rest[pieces:]
    for kind, top, low in weighted_squares(rest[:pieces], scales, 0):
        tops[kind] = top
        lows[kind] = low


def sigma_kernel(pieces, where, scales, tops, lows, *rest):
    lesser, greater, token, held, sems = rest[-5:]
    token[...] = jnp.zeros_like(token)
    copies = []
    for kind, top, low in weighted_squares(rest[:pieces], scales, 1):
        out = greater if kind else lesser
        top = (top + tops[kind]).astype(BF16)
        low = (low + lows[kind]).astype(BF16)
        half = low.shape[1]
        held[kind, 0, :half] = top[:half]
        held[kind, 1, :half] = top[half:]
        rows = slice(0, half)
        copies.append(load(held.at[kind, :, rows], out.at[where[0], :, rows], sems.at[kind, 0]))
        held[kind, 0, half:, half:] = low[:half]
        held[kind, 1, half:, half:] = low[half:]
        held[kind, 0, half:, :half] = jnp.transpose(top[:half, half:])
        held[kind, 1, half:, :half] = -jnp.transpose(top[half:, half:])
        rows = slice(half, 2 * half)
        copies.append(load(held.at[kind, :, rows], out.at[where[0], :, rows], sems.at[kind, 1]))
    for copy in copies:
        copy.wait()


def whole(count):
    return [pl.BlockSpec(memory_space=pltpu.VMEM)] * count


SCALAR = pl.BlockSpec(memory_space=pltpu.SMEM)
FAR = pl.BlockSpec(memory_space=pltpu.HBM)
NEAR = pl.BlockSpec(memory_space=pltpu.VMEM)


def call(kernel, outs, specs, args, scratch=()):
    return pl.pallas_call(
        kernel,
        out_shape=outs,
        in_specs=specs,
        out_specs=[NEAR] * len(outs),
        scratch_shapes=list(scratch),
        compiler_params=pltpu.CompilerParams(vmem_limit_bytes=24 * 2**20),
        cost_estimate=pl.CostEstimate(flops=1000, bytes_accessed=1000, transcendentals=0),
    )(*args)


def self_blocks(where, scales, own, other, blocks, previous):
    rows = sum(part.shape[0] for part in own)
    pieces = len(own)
    sums = call(
        functools.partial(own_sigma_kernel, pieces),
        [
            jax.ShapeDtypeStruct((2, rows, rows), F32),
            jax.ShapeDtypeStruct((2, rows, rows // 2), F32),
        ],
        [NEAR] * (1 + pieces),
        (scales, *own),
    )
    return pl.pallas_call(
        functools.partial(sigma_kernel, pieces),
        out_shape=[jax.ShapeDtypeStruct(blocks, BF16)] * 2 + [jax.ShapeDtypeStruct((8, 128), F32)],
        in_specs=[SCALAR] + [NEAR] * (3 + pieces) + [pl.BlockSpec(memory_space=pl.ANY)] * len(previous),
        out_specs=[pl.BlockSpec(memory_space=pl.ANY)] * 2 + [NEAR],
        scratch_shapes=[
            pltpu.VMEM((2, 2, rows, rows), BF16),
            pltpu.SemaphoreType.DMA((2, 2)),
        ],
        input_output_aliases={4 + pieces + at: at for at in range(len(previous))},
        compiler_params=pltpu.CompilerParams(vmem_limit_bytes=24 * 2**20),
        cost_estimate=pl.CostEstimate(flops=1000, bytes_accessed=1000, transcendentals=0),
    )(where, scales, *sums, *other, *previous)


def body(energies, chips, precond, coupling, source, sigma_ret, occupation, shift_offsets, shift_weights):
    _, slabs, _, rows, modes = source.shape
    width = 2 * modes
    energy, chip = lax.axis_index("energy"), lax.axis_index("space")
    odd = lax.rem(chip, 2)
    inner = jnp.logical_and(chip > 0, chip < chips - 1).astype(jnp.int32)
    if LEAD_A:
        lead, valid = 1 - odd, [jnp.ones_like(inner), inner]
    else:
        lead, valid = odd, [inner, jnp.ones_like(inner)]
    where = jnp.stack([lead, *valid, energy]).astype(jnp.int32)

    def at(e, c):
        return e * chips + c

    pairing_a, pairing_b = [], []
    for e in range(energies):
        for c in range(chips):
            pairing_a.append((at(e, c), at(e, c ^ 1)))
            if 0 < c < chips - 1:
                pairing_b.append((at(e, c), at(e, ((c + 1) ^ 1) - 1)))
            else:
                pairing_b.append((at(e, c), at(e ^ 1, c)))
    pairings = (pairing_a, pairing_b) if LEAD_A else (pairing_b, pairing_a)
    swap = [(at(e, c), at(e ^ 1, c)) for e in range(energies) for c in range(chips)]

    precond, source, sigma = precond[0], source[0], sigma_ret[0]
    pair = jax.ShapeDtypeStruct((rows, width), BF16)
    total = jax.ShapeDtypeStruct((rows, width), F32)
    matrix = jax.ShapeDtypeStruct((2, rows, rows), BF16)
    drive = jax.ShapeDtypeStruct((2, rows, modes), F32)
    states, arrived = [None, None], [None, None]
    owns, drives = [None, None], [None, None]

    precond, coupling, source = [
        pltpu.with_memory_space_constraint(array, pltpu.HBM) for array in (precond, coupling, source)
    ]
    states[0], send, owns[0], link, drives[0] = call(
        lead_kernel,
        [pair, pair, matrix, matrix, drive],
        [SCALAR, FAR, FAR, FAR],
        (where, precond, coupling, source),
        [pltpu.SemaphoreType.DMA((5,))],
    )
    arrived[0] = lax.ppermute(send, AXES, pairings[0])
    states[1], send, owns[1], within, drives[1], chain, term = call(
        trail_kernel,
        [pair, pair, matrix, matrix, drive, matrix, total],
        [SCALAR, FAR, FAR, FAR] + [NEAR] * 3,
        (where, precond, coupling, source, link, owns[0], states[0]),
        [pltpu.SemaphoreType.DMA((4,))],
    )
    arrived[1] = lax.ppermute(send, AXES, pairings[1])
    for sweep in range(1, SWEEPS):
        first, last = sweep == 1, sweep == SWEEPS - 1
        kind = "first" if first else "holding" if HOLD else "plain"
        extra_out = {"first": [jax.ShapeDtypeStruct((width, 8), F32)], "holding": [pair], "plain": []}
        extra_in = {"first": (occupation, shift_offsets, shift_weights), "holding": (send,) if not first else (), "plain": ()}
        if kind == "plain":
            arrived[1] = lax.ppermute(send, AXES, pairings[1])
        bases = call(
            functools.partial(base_kernel, kind),
            [total, total] + extra_out[kind],
            [SCALAR] + [NEAR] * 9 + [NEAR, SCALAR, SCALAR][: len(extra_in[kind])],
            (where, within, sigma, *owns, *drives, *states, term) + extra_in[kind],
        )
        if first:
            scales = bases[2]
        elif kind == "holding":
            arrived[1] = lax.ppermute(bases[2], AXES, pairings[1])
        states, blocks, token = list(states), [], []
        for side in range(2):
            if last:
                pieces = 1 if side else LEAD_PIECES
                outs = [jax.ShapeDtypeStruct((rows // pieces, width), BF16)] * pieces
            else:
                outs = [pair, pair]
            extra = token if last else [term] * side
            results = call(
                functools.partial(step_kernel, side, last, len(outs)),
                outs,
                [SCALAR] + [NEAR] * (5 + len(extra)),
                (where, owns[side], chain, link, bases[side], arrived[side], *extra),
            )
            if last:
                others = [lax.ppermute(result, AXES, swap) for result in results]
                slab = (1 - lead if side else lead)[None].astype(jnp.int32)
                *blocks, after = self_blocks(
                    slab, scales, results, others, (slabs, 2, rows, rows), blocks
                )
                token = [after]
                continue
            states[side], send = results
            if not side:
                arrived[0] = lax.ppermute(send, AXES, pairings[0])
                (term,) = call(
                    term_kernel, [total], [SCALAR, NEAR, NEAR], (where, within, states[0])
                )
    return tuple(block[None] for block in blocks)


def solution(mesh):
    energies, chips = mesh.shape["energy"], mesh.shape["space"]
    placed = (
        P("energy", "space", None, None, None),
        P("space", None, None, None),
        P("energy", "space", None, None, None),
        P("energy", "space", None, None),
        P(),
        P(),
        P(),
    )
    return jax.shard_map(
        functools.partial(body, energies, chips),
        mesh=mesh,
        in_specs=placed,
        out_specs=(P("energy", "space", None, None, None), P("energy", "space", None, None, None)),
        check_vma=False,
    )
```

```python
import functools

import jax
import jax.numpy as jnp
from jax import lax
from jax.experimental import pallas as pl
from jax.experimental.pallas import tpu as pltpu
from jax.sharding import PartitionSpec as P

SWEEPS = 4
F32 = jnp.float32
BF16 = jnp.bfloat16
AXES = ("energy", "space")
LEAD_A = True
LEAD_PIECES = 2
HELD = {1: (0, 2), 2: (0, 2), 3: (2, 2)}


def times_i(pair, sign):
    half = pair.shape[1] // 2
    real, imag = pair[:, :half], pair[:, half:]
    if sign > 0:
        return jnp.concatenate([-imag, real], axis=1)
    return jnp.concatenate([imag, -real], axis=1)


def product(matrix, pair):
    out = jnp.dot(matrix[0], pair, preferred_element_type=F32)
    return out + jnp.dot(matrix[1], times_i(pair, 1), preferred_element_type=F32)


def transposed_dot(matrix, pair):
    return lax.dot_general(matrix, pair, (((0,), (0,)), ((), ())), preferred_element_type=F32)


def adjoint(matrix, pair):
    out = transposed_dot(matrix[0], pair)
    return out + transposed_dot(matrix[1], times_i(pair, -1))


def joined(ref, slab):
    return jnp.concatenate([ref[slab, 0], ref[slab, 1]], axis=1)


def load(source, held, sem):
    copy = pltpu.make_async_copy(source, held, sem)
    copy.start()
    return copy


def lead_kernel(where, precond, coupling, source, states, send, own, link, drive, sems):
    slab = where[0]
    copies = [
        load(source.at[slab], drive, sems.at[0]),
        load(precond.at[slab, 0], own.at[0], sems.at[1]),
        load(precond.at[slab, 1], own.at[1], sems.at[2]),
        load(coupling.at[1, 0], link.at[0], sems.at[3]),
        load(coupling.at[1, 1], link.at[1], sems.at[4]),
    ]
    copies[0].wait()
    pair = jnp.concatenate([drive[0], drive[1]], axis=1).astype(BF16)
    copies[1].wait()
    partial = jnp.dot(own[0], pair, preferred_element_type=F32)
    copies[2].wait()
    partial = partial + jnp.dot(own[1], times_i(pair, 1), preferred_element_type=F32)
    fresh = partial.astype(BF16)
    states[...] = fresh
    copies[3].wait()

    @pl.when(slab == 0)
    def _():
        send[...] = fresh
        copies[4].wait()

    @pl.when(slab == 1)
    def _():
        handed = transposed_dot(link[0], fresh)
        copies[4].wait()
        send[...] = (handed + transposed_dot(link[1], times_i(fresh, -1))).astype(BF16)


def trail_kernel(
    where, precond, coupling, source, link, lead, lead_states,
    states, send, own, inner, drive, chain, term, sems,
):
    slab = 1 - where[0]
    copies = [
        load(source.at[slab], drive, sems.at[0]),
        load(precond.at[slab, 0], own.at[0], sems.at[1]),
        load(precond.at[slab, 1], own.at[1], sems.at[2]),
        load(coupling.at[0], inner, sems.at[3]),
    ]
    copies[0].wait()
    pair = jnp.concatenate([drive[0], drive[1]], axis=1).astype(BF16)
    copies[1].wait()
    partial = jnp.dot(own[0], pair, preferred_element_type=F32)
    copies[2].wait()
    partial = partial + jnp.dot(own[1], times_i(pair, 1), preferred_element_type=F32)
    fresh = partial.astype(BF16)
    states[...] = fresh
    send_fresh(slab, link, fresh, send)

    def write_chain(matrix):
        both = product(matrix, jnp.concatenate([link[0], link[1]], axis=1))
        half = both.shape[1] // 2
        chain[0] = both[:, :half].astype(BF16)
        chain[1] = both[:, half:].astype(BF16)

    @pl.when(slab == 1)
    def _():
        write_chain(own)

    @pl.when(slab == 0)
    def _():
        write_chain(lead)

    copies[3].wait()
    write_term(slab, inner, lead_states, term)


def send_fresh(slab, link, fresh, send):
    @pl.when(slab == 1)
    def _():
        send[...] = adjoint(link, fresh).astype(BF16)

    @pl.when(slab == 0)
    def _():
        send[...] = fresh


def write_term(slab, inner, states, term):
    @pl.when(slab == 0)
    def _():
        term[...] = product(inner, states[...])

    @pl.when(slab == 1)
    def _():
        term[...] = adjoint(inner, states[...]).astype(BF16).astype(F32)


def hand_kernel(where, chain, link, hand):
    @pl.when(where[0] == 0)
    def _():
        both = adjoint(link, jnp.concatenate([chain[0], chain[1]], axis=1))
        half = both.shape[1] // 2
        hand[0] = both[:, :half].astype(BF16)
        hand[1] = both[:, half:].astype(BF16)


def base_kernel(
    kind, held, last, where, inner, link, sigma, own_a, own_b, source_a, source_b, states_a, states_b, term, *rest
):
    if kind == "before":
        base_a, base_b, base_send, send = rest[-4:]
        send[...] = rest[0][...]
    else:
        base_a, base_b, base_send = rest[-3:]
    parts = jnp.where(lax.rem(where[3], 2) == 0, held[0], held[1])
    here_a, here_b = parts > 0, parts > 1
    if kind == "after":
        here_a, here_b = jnp.logical_not(here_a), jnp.logical_not(here_b)

    def local(slab, source, states):
        rows = states.shape[0]
        padded = jnp.concatenate([sigma[slab], jnp.zeros((6, rows), F32)], axis=0)
        columns = jnp.transpose(padded)
        real, imag = columns[:, 0:1], columns[:, 1:2]
        wide = states[...].astype(F32)
        half = wide.shape[1] // 2
        turned = jnp.concatenate([-wide[:, half:], wide[:, :half]], axis=1)
        drive = jnp.concatenate([source[0], source[1]], axis=1)
        return drive + (real * wide + imag * turned)

    @pl.when(jnp.logical_and(here_a, where[0] == 1))
    def _():
        handed = adjoint(inner, states_b[...]).astype(BF16).astype(F32)
        base_a[...] = product(own_a, (local(1, source_a, states_a) + handed).astype(BF16))

    @pl.when(jnp.logical_and(here_a, where[0] == 0))
    def _():
        base_a[...] = local(0, source_a, states_a) + product(inner, states_b[...])

    @pl.when(jnp.logical_and(here_b, where[0] == 1))
    def _():
        base_b[...] = local(0, source_b, states_b) + term[...]

    @pl.when(jnp.logical_and(here_b, where[0] == 0))
    def _():
        driven = (local(1, source_b, states_b) + term[...]).astype(BF16)
        solved = product(own_b, driven)
        base_b[...] = solved
        if not last:
            base_send[...] = adjoint(link, solved.astype(BF16))


def scales_kernel(where, occupation, offsets, weights, scales):
    energy = where[3]
    modes = occupation.shape[1]
    rows = []
    for at, target in ((0, energy), (1, 1 - energy)):
        total = jnp.float32(0)
        for shift in range(offsets.shape[1]):
            reached = energy + offsets[energy, shift] == target
            total = total + jnp.where(reached, weights[energy, shift], jnp.float32(0))
        weight = jnp.full((1, modes), total, F32) / modes
        filled = occupation[pl.ds(target, 1), :]
        for kind, share in ((0, filled), (1, 1.0 - filled)):
            row = weight * share
            rows.append(jnp.concatenate([row, row], axis=1))
    rows = jnp.concatenate(rows + [jnp.zeros((8 - len(rows), 2 * modes), F32)], axis=0)
    scales[...] = jnp.transpose(rows)


def step_kernel(side, last, outs, where, own, chain, link, base, arrived, *rest):
    results = rest[len(rest) - outs :]
    slab = 1 - where[0] if side else where[0]

    def message():
        return jnp.where(where[1 + side] != 0, arrived[...], jnp.zeros_like(arrived))

    def keep(fresh):
        if not last:
            results[0][...] = fresh
            return
        rows = fresh.shape[0] // outs
        for at, piece in enumerate(results):
            piece[...] = fresh[at * rows : (at + 1) * rows]

    @pl.when(slab == 1)
    def _():
        fresh = (base[...] + product(chain, message())).astype(BF16)
        keep(fresh)
        if side and not last:
            hand, base_send = rest[:2]
            results[1][...] = (base_send[...] + product(hand, message())).astype(BF16)
        elif not last:
            results[1][...] = adjoint(link, fresh).astype(BF16)

    @pl.when(slab == 0)
    def _():
        driven = (base[...] + message().astype(F32)).astype(BF16)
        fresh = product(own, driven).astype(BF16)
        keep(fresh)
        if not last:
            results[1][...] = fresh

    if not side and not last:
        write_term(1 - slab, rest[0], results[0], results[2])


def weighted_squares(parts, scales, at):
    pair = jnp.concatenate([part[...] for part in parts], axis=0)
    half = pair.shape[0] // 2
    turned = times_i(pair, -1)
    upper = jnp.concatenate([pair[:half], turned[:half]], axis=0)
    lower = jnp.concatenate([pair[half:], turned[half:]], axis=0)
    wide = jnp.transpose(pair).astype(F32)
    for kind in range(2):
        weighted = (wide * scales[:, 2 * at + kind : 2 * at + kind + 1]).astype(BF16)
        yield (
            kind,
            jnp.dot(upper, weighted, preferred_element_type=F32),
            jnp.dot(lower, weighted[:, half:], preferred_element_type=F32),
        )


def own_sigma_kernel(pieces, scales, *rest):
    tops, lows = rest[pieces:]
    for kind, top, low in weighted_squares(rest[:pieces], scales, 0):
        tops[kind] = top
        lows[kind] = low


def sigma_kernel(pieces, where, scales, tops, lows, *rest):
    lesser, greater, token, held, sems = rest[-5:]
    token[...] = jnp.zeros_like(token)
    copies = []
    for kind, top, low in weighted_squares(rest[:pieces], scales, 1):
        out = greater if kind else lesser
        top = (top + tops[kind]).astype(BF16)
        low = (low + lows[kind]).astype(BF16)
        half = low.shape[1]
        held[kind, 0, :half] = top[:half]
        held[kind, 1, :half] = top[half:]
        rows = slice(0, half)
        copies.append(load(held.at[kind, :, rows], out.at[where[0], :, rows], sems.at[kind, 0]))
        held[kind, 0, half:, half:] = low[:half]
        held[kind, 1, half:, half:] = low[half:]
        held[kind, 0, half:, :half] = jnp.transpose(top[:half, half:])
        held[kind, 1, half:, :half] = -jnp.transpose(top[half:, half:])
        rows = slice(half, 2 * half)
        copies.append(load(held.at[kind, :, rows], out.at[where[0], :, rows], sems.at[kind, 1]))
    for copy in copies:
        copy.wait()


def whole(count):
    return [pl.BlockSpec(memory_space=pltpu.VMEM)] * count


SCALAR = pl.BlockSpec(memory_space=pltpu.SMEM)
FAR = pl.BlockSpec(memory_space=pltpu.HBM)
NEAR = pl.BlockSpec(memory_space=pltpu.VMEM)


def call(kernel, outs, specs, args, scratch=(), aliases=None):
    scalars, specs, args = (args[0], specs[1:], args[1:]) if specs[0] is SCALAR else ((), specs, args)
    count = len(scalars)
    aliases = {count - 1 + source: target for source, target in (aliases or {}).items()}

    def unpacked(*refs):
        if count:
            kernel([ref[0] for ref in refs[:count]], *refs[count:])
        else:
            kernel(*refs)

    specs, args = [SCALAR] * count + list(specs), (*scalars, *args)
    return pl.pallas_call(
        unpacked,
        out_shape=outs,
        in_specs=specs,
        out_specs=[NEAR] * len(outs),
        scratch_shapes=list(scratch),
        input_output_aliases=aliases,
        compiler_params=pltpu.CompilerParams(vmem_limit_bytes=24 * 2**20),
        cost_estimate=pl.CostEstimate(flops=1000, bytes_accessed=1000, transcendentals=0),
    )(*args)


def self_blocks(where, scales, own, other, blocks, previous):
    rows = sum(part.shape[0] for part in own)
    pieces = len(own)
    sums = call(
        functools.partial(own_sigma_kernel, pieces),
        [
            jax.ShapeDtypeStruct((2, rows, rows), F32),
            jax.ShapeDtypeStruct((2, rows, rows // 2), F32),
        ],
        [NEAR] * (1 + pieces),
        (scales, *own),
    )
    return pl.pallas_call(
        functools.partial(sigma_kernel, pieces),
        out_shape=[jax.ShapeDtypeStruct(blocks, BF16)] * 2 + [jax.ShapeDtypeStruct((8, 128), F32)],
        in_specs=[SCALAR] + [NEAR] * (3 + pieces) + [pl.BlockSpec(memory_space=pl.ANY)] * len(previous),
        out_specs=[pl.BlockSpec(memory_space=pl.ANY)] * 2 + [NEAR],
        scratch_shapes=[
            pltpu.VMEM((2, 2, rows, rows), BF16),
            pltpu.SemaphoreType.DMA((2, 2)),
        ],
        input_output_aliases={4 + pieces + at: at for at in range(len(previous))},
        compiler_params=pltpu.CompilerParams(vmem_limit_bytes=24 * 2**20),
        cost_estimate=pl.CostEstimate(flops=1000, bytes_accessed=1000, transcendentals=0),
    )(where, scales, *sums, *other, *previous)


def body(energies, chips, precond, coupling, source, sigma_ret, occupation, shift_offsets, shift_weights):
    _, slabs, _, rows, modes = source.shape
    width = 2 * modes
    energy, chip = lax.axis_index("energy"), lax.axis_index("space")
    odd = lax.rem(chip, 2)
    inner = jnp.logical_and(chip > 0, chip < chips - 1).astype(jnp.int32)
    if LEAD_A:
        lead, valid = 1 - odd, [jnp.ones_like(inner), inner]
    else:
        lead, valid = odd, [inner, jnp.ones_like(inner)]
    where = [jnp.reshape(value, (1,)).astype(jnp.int32) for value in (lead, *valid, energy)]

    def at(e, c):
        return e * chips + c

    pairing_a, pairing_b = [], []
    for e in range(energies):
        for c in range(chips):
            pairing_a.append((at(e, c), at(e, c ^ 1)))
            if 0 < c < chips - 1:
                pairing_b.append((at(e, c), at(e, ((c + 1) ^ 1) - 1)))
            else:
                pairing_b.append((at(e, c), at(e ^ 1, c)))
    pairings = (pairing_a, pairing_b) if LEAD_A else (pairing_b, pairing_a)
    swap = [(at(e, c), at(e ^ 1, c)) for e in range(energies) for c in range(chips)]

    precond, source, sigma = precond[0], source[0], sigma_ret[0]
    pair = jax.ShapeDtypeStruct((rows, width), BF16)
    total = jax.ShapeDtypeStruct((rows, width), F32)
    matrix = jax.ShapeDtypeStruct((2, rows, rows), BF16)
    drive = jax.ShapeDtypeStruct((2, rows, modes), F32)
    states, arrived = [None, None], [None, None]
    owns, drives = [None, None], [None, None]

    precond, coupling, source = [
        pltpu.with_memory_space_constraint(array, pltpu.HBM) for array in (precond, coupling, source)
    ]
    states[0], send, owns[0], link, drives[0] = call(
        lead_kernel,
        [pair, pair, matrix, matrix, drive],
        [SCALAR, FAR, FAR, FAR],
        (where, precond, coupling, source),
        [pltpu.SemaphoreType.DMA((5,))],
    )
    arrived[0] = lax.ppermute(send, AXES, pairings[0])
    states[1], send, owns[1], within, drives[1], chain, term = call(
        trail_kernel,
        [pair, pair, matrix, matrix, drive, matrix, total],
        [SCALAR, FAR, FAR, FAR] + [NEAR] * 3,
        (where, precond, coupling, source, link, owns[0], states[0]),
        [pltpu.SemaphoreType.DMA((4,))],
    )
    for sweep in range(1, SWEEPS):
        first, last = sweep == 1, sweep == SWEEPS - 1
        common = (where, within, link, sigma, *owns, *drives, *states, term)
        near = [SCALAR] + [NEAR] * 10
        *bases, send = call(
            functools.partial(base_kernel, "before", HELD[sweep], last),
            [total, total, total, pair],
            near + [NEAR],
            common + (send,),
        )
        arrived[1] = lax.ppermute(send, AXES, pairings[1])
        bases = call(
            functools.partial(base_kernel, "after", HELD[sweep], last),
            [total, total, total],
            near + [NEAR] * 3,
            common + tuple(bases),
            aliases={11: 0, 12: 1, 13: 2},
        )
        states, blocks, token = list(states), [], []
        for side in range(2):
            if last:
                pieces = 1 if side else LEAD_PIECES
                outs = [jax.ShapeDtypeStruct((rows // pieces, width), BF16)] * pieces
            else:
                outs = [pair, pair] if side else [pair, pair, total]
            if last:
                extra = token
            elif side:
                extra = [hand, bases[2]]
            else:
                extra = [within]
            results = call(
                functools.partial(step_kernel, side, last, len(outs)),
                outs,
                [SCALAR] + [NEAR] * (5 + len(extra)),
                (where, owns[side], chain, link, bases[side], arrived[side], *extra),
            )
            if last:
                others = [lax.ppermute(result, AXES, swap) for result in results]
                slab = (1 - lead if side else lead)[None].astype(jnp.int32)
                *blocks, after = self_blocks(
                    slab, scales, results, others, (slabs, 2, rows, rows), blocks
                )
                token = [after]
                continue
            states[side], send = results[:2]
            if not side:
                arrived[0] = lax.ppermute(send, AXES, pairings[0])
                term = results[2]
                if first:
                    (hand,) = call(
                        hand_kernel, [matrix], [SCALAR, NEAR, NEAR], (where, chain, link)
                    )
                else:
                    (scales,) = call(
                        scales_kernel,
                        [jax.ShapeDtypeStruct((width, 8), F32)],
                        [SCALAR, NEAR, SCALAR, SCALAR],
                        (where, occupation, shift_offsets, shift_weights),
                    )
    return tuple(block[None] for block in blocks)


def solution(mesh):
    energies, chips = mesh.shape["energy"], mesh.shape["space"]
    placed = (
        P("energy", "space", None, None, None),
        P("space", None, None, None),
        P("energy", "space", None, None, None),
        P("energy", "space", None, None),
        P(),
        P(),
        P(),
    )
    return jax.shard_map(
        functools.partial(body, energies, chips),
        mesh=mesh,
        in_specs=placed,
        out_specs=(P("energy", "space", None, None, None), P("energy", "space", None, None, None)),
        check_vma=False,
    )
```

```python
import functools

import jax
import jax.numpy as jnp
from jax import lax
from jax.experimental import pallas as pl
from jax.experimental.pallas import tpu as pltpu
from jax.sharding import PartitionSpec as P

SWEEPS = 4
F32 = jnp.float32
BF16 = jnp.bfloat16
AXES = ("energy", "space")
LEAD_A = True
LEAD_PIECES = 2
HELD = {1: (0, 2), 2: (0, 2), 3: (2, 1)}


def times_i(pair, sign):
    half = pair.shape[1] // 2
    real, imag = pair[:, :half], pair[:, half:]
    if sign > 0:
        return jnp.concatenate([-imag, real], axis=1)
    return jnp.concatenate([imag, -real], axis=1)


def product(matrix, pair):
    out = jnp.dot(matrix[0], pair, preferred_element_type=F32)
    return out + jnp.dot(matrix[1], times_i(pair, 1), preferred_element_type=F32)


def transposed_dot(matrix, pair):
    return lax.dot_general(matrix, pair, (((0,), (0,)), ((), ())), preferred_element_type=F32)


def adjoint(matrix, pair):
    out = transposed_dot(matrix[0], pair)
    return out + transposed_dot(matrix[1], times_i(pair, -1))


def joined(ref, slab):
    return jnp.concatenate([ref[slab, 0], ref[slab, 1]], axis=1)


def load(source, held, sem):
    copy = pltpu.make_async_copy(source, held, sem)
    copy.start()
    return copy


def lead_kernel(where, precond, coupling, source, states, send, own, link, drive, sems):
    slab = where[0]
    copies = [
        load(source.at[slab], drive, sems.at[0]),
        load(precond.at[slab, 0], own.at[0], sems.at[1]),
        load(precond.at[slab, 1], own.at[1], sems.at[2]),
        load(coupling.at[1, 0], link.at[0], sems.at[3]),
        load(coupling.at[1, 1], link.at[1], sems.at[4]),
    ]
    copies[0].wait()
    pair = jnp.concatenate([drive[0], drive[1]], axis=1).astype(BF16)
    copies[1].wait()
    partial = jnp.dot(own[0], pair, preferred_element_type=F32)
    copies[2].wait()
    partial = partial + jnp.dot(own[1], times_i(pair, 1), preferred_element_type=F32)
    fresh = partial.astype(BF16)
    states[...] = fresh
    copies[3].wait()

    @pl.when(slab == 0)
    def _():
        send[...] = fresh
        copies[4].wait()

    @pl.when(slab == 1)
    def _():
        handed = transposed_dot(link[0], fresh)
        copies[4].wait()
        send[...] = (handed + transposed_dot(link[1], times_i(fresh, -1))).astype(BF16)


def trail_kernel(
    where, precond, coupling, source, link, lead, lead_states,
    states, send, own, inner, drive, chain, term, sems,
):
    slab = 1 - where[0]
    copies = [
        load(source.at[slab], drive, sems.at[0]),
        load(precond.at[slab, 0], own.at[0], sems.at[1]),
        load(precond.at[slab, 1], own.at[1], sems.at[2]),
        load(coupling.at[0], inner, sems.at[3]),
    ]
    copies[0].wait()
    pair = jnp.concatenate([drive[0], drive[1]], axis=1).astype(BF16)
    copies[1].wait()
    partial = jnp.dot(own[0], pair, preferred_element_type=F32)
    copies[2].wait()
    partial = partial + jnp.dot(own[1], times_i(pair, 1), preferred_element_type=F32)
    fresh = partial.astype(BF16)
    states[...] = fresh
    send_fresh(slab, link, fresh, send)

    def write_chain(matrix):
        both = product(matrix, jnp.concatenate([link[0], link[1]], axis=1))
        half = both.shape[1] // 2
        chain[0] = both[:, :half].astype(BF16)
        chain[1] = both[:, half:].astype(BF16)

    @pl.when(slab == 1)
    def _():
        write_chain(own)

    @pl.when(slab == 0)
    def _():
        write_chain(lead)

    copies[3].wait()
    write_term(slab, inner, lead_states, term)


def send_fresh(slab, link, fresh, send):
    @pl.when(slab == 1)
    def _():
        send[...] = adjoint(link, fresh).astype(BF16)

    @pl.when(slab == 0)
    def _():
        send[...] = fresh


def write_term(slab, inner, states, term):
    @pl.when(slab == 0)
    def _():
        term[...] = product(inner, states[...])

    @pl.when(slab == 1)
    def _():
        term[...] = adjoint(inner, states[...]).astype(BF16).astype(F32)


def hand_kernel(where, chain, link, hand):
    @pl.when(where[0] == 0)
    def _():
        both = adjoint(link, jnp.concatenate([chain[0], chain[1]], axis=1))
        half = both.shape[1] // 2
        hand[0] = both[:, :half].astype(BF16)
        hand[1] = both[:, half:].astype(BF16)


def base_kernel(
    kind, held, last, where, inner, link, sigma, own_a, own_b, source_a, source_b, states_a, states_b, term, *rest
):
    if kind == "before":
        base_a, base_b, base_send, send = rest[-4:]
        send[...] = rest[0][...]
    else:
        base_a, base_b, base_send = rest[-3:]
    parts = jnp.where(lax.rem(where[3], 2) == 0, held[0], held[1])
    here_a, here_b = parts > 0, parts > 1
    if kind == "after":
        here_a, here_b = jnp.logical_not(here_a), jnp.logical_not(here_b)

    def local(slab, source, states):
        rows = states.shape[0]
        padded = jnp.concatenate([sigma[slab], jnp.zeros((6, rows), F32)], axis=0)
        columns = jnp.transpose(padded)
        real, imag = columns[:, 0:1], columns[:, 1:2]
        wide = states[...].astype(F32)
        half = wide.shape[1] // 2
        turned = jnp.concatenate([-wide[:, half:], wide[:, :half]], axis=1)
        drive = jnp.concatenate([source[0], source[1]], axis=1)
        return drive + (real * wide + imag * turned)

    @pl.when(jnp.logical_and(here_a, where[0] == 1))
    def _():
        handed = adjoint(inner, states_b[...]).astype(BF16).astype(F32)
        base_a[...] = product(own_a, (local(1, source_a, states_a) + handed).astype(BF16))

    @pl.when(jnp.logical_and(here_a, where[0] == 0))
    def _():
        base_a[...] = local(0, source_a, states_a) + product(inner, states_b[...])

    @pl.when(jnp.logical_and(here_b, where[0] == 1))
    def _():
        base_b[...] = local(0, source_b, states_b) + term[...]

    @pl.when(jnp.logical_and(here_b, where[0] == 0))
    def _():
        driven = (local(1, source_b, states_b) + term[...]).astype(BF16)
        solved = product(own_b, driven)
        base_b[...] = solved
        if not last:
            base_send[...] = adjoint(link, solved.astype(BF16))


def scales_kernel(where, occupation, offsets, weights, scales):
    energy = where[3]
    modes = occupation.shape[1]
    rows = []
    for at, target in ((0, energy), (1, 1 - energy)):
        total = jnp.float32(0)
        for shift in range(offsets.shape[1]):
            reached = energy + offsets[energy, shift] == target
            total = total + jnp.where(reached, weights[energy, shift], jnp.float32(0))
        weight = jnp.full((1, modes), total, F32) / modes
        filled = occupation[pl.ds(target, 1), :]
        for kind, share in ((0, filled), (1, 1.0 - filled)):
            row = weight * share
            rows.append(jnp.concatenate([row, row], axis=1))
    rows = jnp.concatenate(rows + [jnp.zeros((8 - len(rows), 2 * modes), F32)], axis=0)
    scales[...] = jnp.transpose(rows)


def step_kernel(side, last, outs, where, own, chain, link, base, arrived, *rest):
    results = rest[len(rest) - outs :]
    slab = 1 - where[0] if side else where[0]

    def message():
        return jnp.where(where[1 + side] != 0, arrived[...], jnp.zeros_like(arrived))

    def keep(fresh):
        if not last:
            results[0][...] = fresh
            return
        rows = fresh.shape[0] // outs
        for at, piece in enumerate(results):
            piece[...] = fresh[at * rows : (at + 1) * rows]

    @pl.when(slab == 1)
    def _():
        fresh = (base[...] + product(chain, message())).astype(BF16)
        keep(fresh)
        if side and not last:
            hand, base_send = rest[:2]
            results[1][...] = (base_send[...] + product(hand, message())).astype(BF16)
        elif not last:
            results[1][...] = adjoint(link, fresh).astype(BF16)

    @pl.when(slab == 0)
    def _():
        driven = (base[...] + message().astype(F32)).astype(BF16)
        fresh = product(own, driven).astype(BF16)
        keep(fresh)
        if not last:
            results[1][...] = fresh

    if not side and not last:
        write_term(1 - slab, rest[0], results[0], results[2])


def squares_inputs(parts):
    pair = jnp.concatenate([part[...] for part in parts], axis=0)
    return (pair, times_i(pair, -1)), jnp.transpose(pair).astype(F32)


def own_sigma_kernel(pieces, scales, *rest):
    tops, lows = rest[pieces:]
    lefts, wide = squares_inputs(rest[:pieces])
    half = wide.shape[1] // 2
    upper = jnp.concatenate([left[:half] for left in lefts], axis=0)
    lower = jnp.concatenate([left[half:] for left in lefts], axis=0)
    for kind in range(2):
        weighted = (wide * scales[:, kind : kind + 1]).astype(BF16)
        tops[kind] = jnp.dot(upper, weighted, preferred_element_type=F32)
        lows[kind] = jnp.dot(lower, weighted[:, half:], preferred_element_type=F32)


def sigma_kernel(pieces, aliased, where, scales, tops, lows, *rest):
    lesser, greater, *token, held, sems = rest[pieces + aliased :]
    for ref in token:
        ref[...] = jnp.zeros_like(ref)
    lefts, wide = squares_inputs(rest[:pieces])
    half = wide.shape[1] // 2
    copies = []

    def send(kind, out, part, at):
        rows = slice(at * half, (at + 1) * half)
        copies.append(
            load(held.at[kind, part, rows], out.at[where[0], part, rows], sems.at[kind, 2 * part + at])
        )

    for kind, out in ((0, lesser), (1, greater)):
        weighted = (wide * scales[:, 2 + kind : 3 + kind]).astype(BF16)
        corners = []
        for part, left in enumerate(lefts):
            rows = slice(part * half, (part + 1) * half)
            top = jnp.dot(left[:half], weighted, preferred_element_type=F32) + tops[kind, rows]
            top = top.astype(BF16)
            held[kind, part, :half] = top
            send(kind, out, part, 0)
            corners.append(top[:, half:])
        for part, left in enumerate(lefts):
            rows = slice(part * half, (part + 1) * half)
            low = jnp.dot(left[half:], weighted[:, half:], preferred_element_type=F32)
            held[kind, part, half:, half:] = (low + lows[kind, rows]).astype(BF16)
            turned = jnp.transpose(corners[part])
            held[kind, part, half:, :half] = -turned if part else turned
            send(kind, out, part, 1)
    for copy in copies:
        copy.wait()


def whole(count):
    return [pl.BlockSpec(memory_space=pltpu.VMEM)] * count


SCALAR = pl.BlockSpec(memory_space=pltpu.SMEM)
FAR = pl.BlockSpec(memory_space=pltpu.HBM)
NEAR = pl.BlockSpec(memory_space=pltpu.VMEM)


def call(kernel, outs, specs, args, scratch=(), aliases=None):
    scalars, specs, args = (args[0], specs[1:], args[1:]) if specs[0] is SCALAR else ((), specs, args)
    count = len(scalars)
    aliases = {count - 1 + source: target for source, target in (aliases or {}).items()}

    def unpacked(*refs):
        if count:
            kernel([ref[0] for ref in refs[:count]], *refs[count:])
        else:
            kernel(*refs)

    specs, args = [SCALAR] * count + list(specs), (*scalars, *args)
    return pl.pallas_call(
        unpacked,
        out_shape=outs,
        in_specs=specs,
        out_specs=[NEAR] * len(outs),
        scratch_shapes=list(scratch),
        input_output_aliases=aliases,
        compiler_params=pltpu.CompilerParams(vmem_limit_bytes=24 * 2**20),
        cost_estimate=pl.CostEstimate(flops=1000, bytes_accessed=1000, transcendentals=0),
    )(*args)


def self_blocks(where, scales, own, other, blocks, previous):
    rows = sum(part.shape[0] for part in own)
    pieces = len(own)
    token = [] if previous else [jax.ShapeDtypeStruct((8, 128), F32)]
    sums = call(
        functools.partial(own_sigma_kernel, pieces),
        [
            jax.ShapeDtypeStruct((2, rows, rows), F32),
            jax.ShapeDtypeStruct((2, rows, rows // 2), F32),
        ],
        [NEAR] * (1 + pieces),
        (scales, *own),
    )
    return pl.pallas_call(
        functools.partial(sigma_kernel, pieces, len(previous)),
        out_shape=[jax.ShapeDtypeStruct(blocks, BF16)] * 2 + token,
        in_specs=[SCALAR] + [NEAR] * (3 + pieces) + [pl.BlockSpec(memory_space=pl.ANY)] * len(previous),
        out_specs=[pl.BlockSpec(memory_space=pl.ANY)] * 2 + [NEAR] * len(token),
        scratch_shapes=[
            pltpu.VMEM((2, 2, rows, rows), BF16),
            pltpu.SemaphoreType.DMA((2, 4)),
        ],
        input_output_aliases={4 + pieces + at: at for at in range(len(previous))},
        compiler_params=pltpu.CompilerParams(vmem_limit_bytes=24 * 2**20),
        cost_estimate=pl.CostEstimate(flops=1000, bytes_accessed=1000, transcendentals=0),
    )(where, scales, *sums, *other, *previous)


def body(energies, chips, precond, coupling, source, sigma_ret, occupation, shift_offsets, shift_weights):
    _, slabs, _, rows, modes = source.shape
    width = 2 * modes
    energy, chip = lax.axis_index("energy"), lax.axis_index("space")
    odd = lax.rem(chip, 2)
    inner = jnp.logical_and(chip > 0, chip < chips - 1).astype(jnp.int32)
    if LEAD_A:
        lead, valid = 1 - odd, [jnp.ones_like(inner), inner]
    else:
        lead, valid = odd, [inner, jnp.ones_like(inner)]
    where = [jnp.reshape(value, (1,)).astype(jnp.int32) for value in (lead, *valid, energy)]

    def at(e, c):
        return e * chips + c

    pairing_a, pairing_b = [], []
    for e in range(energies):
        for c in range(chips):
            pairing_a.append((at(e, c), at(e, c ^ 1)))
            if 0 < c < chips - 1:
                pairing_b.append((at(e, c), at(e, ((c + 1) ^ 1) - 1)))
            else:
                pairing_b.append((at(e, c), at(e ^ 1, c)))
    pairings = (pairing_a, pairing_b) if LEAD_A else (pairing_b, pairing_a)
    swap = [(at(e, c), at(e ^ 1, c)) for e in range(energies) for c in range(chips)]

    precond, source, sigma = precond[0], source[0], sigma_ret[0]
    pair = jax.ShapeDtypeStruct((rows, width), BF16)
    total = jax.ShapeDtypeStruct((rows, width), F32)
    matrix = jax.ShapeDtypeStruct((2, rows, rows), BF16)
    drive = jax.ShapeDtypeStruct((2, rows, modes), F32)
    states, arrived = [None, None], [None, None]
    owns, drives = [None, None], [None, None]

    precond, coupling, source = [
        pltpu.with_memory_space_constraint(array, pltpu.HBM) for array in (precond, coupling, source)
    ]
    states[0], send, owns[0], link, drives[0] = call(
        lead_kernel,
        [pair, pair, matrix, matrix, drive],
        [SCALAR, FAR, FAR, FAR],
        (where, precond, coupling, source),
        [pltpu.SemaphoreType.DMA((5,))],
    )
    arrived[0] = lax.ppermute(send, AXES, pairings[0])
    states[1], send, owns[1], within, drives[1], chain, term = call(
        trail_kernel,
        [pair, pair, matrix, matrix, drive, matrix, total],
        [SCALAR, FAR, FAR, FAR] + [NEAR] * 3,
        (where, precond, coupling, source, link, owns[0], states[0]),
        [pltpu.SemaphoreType.DMA((4,))],
    )
    for sweep in range(1, SWEEPS):
        first, last = sweep == 1, sweep == SWEEPS - 1
        common = (where, within, link, sigma, *owns, *drives, *states, term)
        near = [SCALAR] + [NEAR] * 10
        *bases, send = call(
            functools.partial(base_kernel, "before", HELD[sweep], last),
            [total, total, total, pair],
            near + [NEAR],
            common + (send,),
        )
        arrived[1] = lax.ppermute(send, AXES, pairings[1])
        bases = call(
            functools.partial(base_kernel, "after", HELD[sweep], last),
            [total, total, total],
            near + [NEAR] * 3,
            common + tuple(bases),
            aliases={11: 0, 12: 1, 13: 2},
        )
        states, blocks, token = list(states), [], []
        for side in range(2):
            if last:
                pieces = 1 if side else LEAD_PIECES
                outs = [jax.ShapeDtypeStruct((rows // pieces, width), BF16)] * pieces
            else:
                outs = [pair, pair] if side else [pair, pair, total]
            if last:
                extra = token
            elif side:
                extra = [hand, bases[2]]
            else:
                extra = [within]
            results = call(
                functools.partial(step_kernel, side, last, len(outs)),
                outs,
                [SCALAR] + [NEAR] * (5 + len(extra)),
                (where, owns[side], chain, link, bases[side], arrived[side], *extra),
            )
            if last:
                others = [lax.ppermute(result, AXES, swap) for result in results]
                slab = (1 - lead if side else lead)[None].astype(jnp.int32)
                blocks = self_blocks(slab, scales, results, others, (slabs, 2, rows, rows), blocks)
                blocks, token = blocks[:2], blocks[2:]
                continue
            states[side], send = results[:2]
            if not side:
                arrived[0] = lax.ppermute(send, AXES, pairings[0])
                term = results[2]
                if first:
                    (hand,) = call(
                        hand_kernel, [matrix], [SCALAR, NEAR, NEAR], (where, chain, link)
                    )
                else:
                    (scales,) = call(
                        scales_kernel,
                        [jax.ShapeDtypeStruct((width, 8), F32)],
                        [SCALAR, NEAR, SCALAR, SCALAR],
                        (where, occupation, shift_offsets, shift_weights),
                    )
    return tuple(block[None] for block in blocks)


def solution(mesh):
    energies, chips = mesh.shape["energy"], mesh.shape["space"]
    placed = (
        P("energy", "space", None, None, None),
        P("space", None, None, None),
        P("energy", "space", None, None, None),
        P("energy", "space", None, None),
        P(),
        P(),
        P(),
    )
    return jax.shard_map(
        functools.partial(body, energies, chips),
        mesh=mesh,
        in_specs=placed,
        out_specs=(P("energy", "space", None, None, None), P("energy", "space", None, None, None)),
        check_vma=False,
    )
```

```python
import functools

import jax
import jax.numpy as jnp
from jax import lax
from jax.experimental import pallas as pl
from jax.experimental.pallas import tpu as pltpu
from jax.sharding import PartitionSpec as P

SWEEPS = 4
F32 = jnp.float32
BF16 = jnp.bfloat16
AXES = ("energy", "space")
LEAD_A = True
LEAD_PIECES = 2
HELD = {1: (0, 2), 2: (0, 2), 3: (2, 1)}


def times_i(pair, sign):
    half = pair.shape[1] // 2
    real, imag = pair[:, :half], pair[:, half:]
    if sign > 0:
        return jnp.concatenate([-imag, real], axis=1)
    return jnp.concatenate([imag, -real], axis=1)


def product(matrix, pair):
    out = jnp.dot(matrix[0], pair, preferred_element_type=F32)
    return out + jnp.dot(matrix[1], times_i(pair, 1), preferred_element_type=F32)


def transposed_dot(matrix, pair):
    return lax.dot_general(matrix, pair, (((0,), (0,)), ((), ())), preferred_element_type=F32)


def adjoint(matrix, pair):
    out = transposed_dot(matrix[0], pair)
    return out + transposed_dot(matrix[1], times_i(pair, -1))


def joined(ref, slab):
    return jnp.concatenate([ref[slab, 0], ref[slab, 1]], axis=1)


def load(source, held, sem):
    copy = pltpu.make_async_copy(source, held, sem)
    copy.start()
    return copy


def lead_kernel(where, precond, coupling, source, states, send, own, link, drive, sems):
    slab = where[0]
    copies = [
        load(source.at[slab], drive, sems.at[0]),
        load(precond.at[slab, 0], own.at[0], sems.at[1]),
        load(precond.at[slab, 1], own.at[1], sems.at[2]),
    ]
    links = [pltpu.make_async_copy(coupling.at[1, at], link.at[at], sems.at[3 + at]) for at in range(2)]

    @pl.when(slab == 1)
    def _():
        for copy in links:
            copy.start()

    copies[0].wait()
    pair = jnp.concatenate([drive[0], drive[1]], axis=1).astype(BF16)
    copies[1].wait()
    partial = jnp.dot(own[0], pair, preferred_element_type=F32)
    copies[2].wait()
    partial = partial + jnp.dot(own[1], times_i(pair, 1), preferred_element_type=F32)
    fresh = partial.astype(BF16)
    states[...] = fresh

    @pl.when(slab == 0)
    def _():
        send[...] = fresh

    @pl.when(slab == 1)
    def _():
        links[0].wait()
        handed = transposed_dot(link[0], fresh)
        links[1].wait()
        send[...] = (handed + transposed_dot(link[1], times_i(fresh, -1))).astype(BF16)


def trail_kernel(
    where, precond, coupling, source, given, lead, lead_states,
    states, send, own, inner, drive, chain, term, link, sems,
):
    slab = 1 - where[0]
    copies = [
        load(source.at[slab], drive, sems.at[0]),
        load(precond.at[slab, 0], own.at[0], sems.at[1]),
        load(precond.at[slab, 1], own.at[1], sems.at[2]),
    ]
    missing = pltpu.make_async_copy(coupling.at[1], link, sems.at[4])

    @pl.when(slab == 1)
    def _():
        missing.start()

    copies.append(load(coupling.at[0], inner, sems.at[3]))
    copies[0].wait()
    pair = jnp.concatenate([drive[0], drive[1]], axis=1).astype(BF16)
    copies[1].wait()
    partial = jnp.dot(own[0], pair, preferred_element_type=F32)
    copies[2].wait()
    partial = partial + jnp.dot(own[1], times_i(pair, 1), preferred_element_type=F32)
    fresh = partial.astype(BF16)
    states[...] = fresh

    @pl.when(slab == 1)
    def _():
        missing.wait()

    send_fresh(slab, link, fresh, send)

    def write_chain(matrix):
        both = product(matrix, jnp.concatenate([link[0], link[1]], axis=1))
        half = both.shape[1] // 2
        chain[0] = both[:, :half].astype(BF16)
        chain[1] = both[:, half:].astype(BF16)

    @pl.when(slab == 1)
    def _():
        write_chain(own)

    @pl.when(slab == 0)
    def _():
        write_chain(lead)

    copies[3].wait()
    write_term(slab, inner, lead_states, term)


def send_fresh(slab, link, fresh, send):
    @pl.when(slab == 1)
    def _():
        send[...] = adjoint(link, fresh).astype(BF16)

    @pl.when(slab == 0)
    def _():
        send[...] = fresh


def write_term(slab, inner, states, term):
    @pl.when(slab == 0)
    def _():
        term[...] = product(inner, states[...])

    @pl.when(slab == 1)
    def _():
        term[...] = adjoint(inner, states[...]).astype(BF16).astype(F32)


def hand_kernel(where, chain, link, hand):
    @pl.when(where[0] == 0)
    def _():
        both = adjoint(link, jnp.concatenate([chain[0], chain[1]], axis=1))
        half = both.shape[1] // 2
        hand[0] = both[:, :half].astype(BF16)
        hand[1] = both[:, half:].astype(BF16)


def base_kernel(
    kind, held, last, where, inner, link, sigma, own_a, own_b, source_a, source_b, states_a, states_b, term, *rest
):
    if kind == "before":
        base_a, base_b, base_send, send = rest[-4:]
        send[...] = rest[0][...]
    else:
        base_a, base_b, base_send = rest[-3:]
    parts = jnp.where(lax.rem(where[3], 2) == 0, held[0], held[1])
    here_a, here_b = parts > 0, parts > 1
    if kind == "after":
        here_a, here_b = jnp.logical_not(here_a), jnp.logical_not(here_b)

    def local(slab, source, states):
        rows = states.shape[0]
        padded = jnp.concatenate([sigma[slab], jnp.zeros((6, rows), F32)], axis=0)
        columns = jnp.transpose(padded)
        real, imag = columns[:, 0:1], columns[:, 1:2]
        wide = states[...].astype(F32)
        half = wide.shape[1] // 2
        turned = jnp.concatenate([-wide[:, half:], wide[:, :half]], axis=1)
        drive = jnp.concatenate([source[0], source[1]], axis=1)
        return drive + (real * wide + imag * turned)

    @pl.when(jnp.logical_and(here_a, where[0] == 1))
    def _():
        handed = adjoint(inner, states_b[...]).astype(BF16).astype(F32)
        base_a[...] = product(own_a, (local(1, source_a, states_a) + handed).astype(BF16))

    @pl.when(jnp.logical_and(here_a, where[0] == 0))
    def _():
        base_a[...] = local(0, source_a, states_a) + product(inner, states_b[...])

    @pl.when(jnp.logical_and(here_b, where[0] == 1))
    def _():
        base_b[...] = local(0, source_b, states_b) + term[...]

    @pl.when(jnp.logical_and(here_b, where[0] == 0))
    def _():
        driven = (local(1, source_b, states_b) + term[...]).astype(BF16)
        solved = product(own_b, driven)
        base_b[...] = solved
        if not last:
            base_send[...] = adjoint(link, solved.astype(BF16))


def scales_kernel(where, occupation, offsets, weights, scales):
    energy = where[3]
    modes = occupation.shape[1]
    rows = []
    for at, target in ((0, energy), (1, 1 - energy)):
        total = jnp.float32(0)
        for shift in range(offsets.shape[1]):
            reached = energy + offsets[energy, shift] == target
            total = total + jnp.where(reached, weights[energy, shift], jnp.float32(0))
        weight = jnp.full((1, modes), total, F32) / modes
        filled = occupation[pl.ds(target, 1), :]
        for kind, share in ((0, filled), (1, 1.0 - filled)):
            row = weight * share
            rows.append(jnp.concatenate([row, row], axis=1))
    rows = jnp.concatenate(rows + [jnp.zeros((8 - len(rows), 2 * modes), F32)], axis=0)
    scales[...] = jnp.transpose(rows)


def step_kernel(side, last, outs, where, own, chain, link, base, arrived, *rest):
    results = rest[len(rest) - outs :]
    slab = 1 - where[0] if side else where[0]

    def message():
        return jnp.where(where[1 + side] != 0, arrived[...], jnp.zeros_like(arrived))

    def keep(fresh):
        if not last:
            results[0][...] = fresh
            return
        rows = fresh.shape[0] // outs
        for at, piece in enumerate(results):
            piece[...] = fresh[at * rows : (at + 1) * rows]

    @pl.when(slab == 1)
    def _():
        fresh = (base[...] + product(chain, message())).astype(BF16)
        keep(fresh)
        if side and not last:
            hand, base_send = rest[:2]
            results[1][...] = (base_send[...] + product(hand, message())).astype(BF16)
        elif not last:
            results[1][...] = adjoint(link, fresh).astype(BF16)

    @pl.when(slab == 0)
    def _():
        driven = (base[...] + message().astype(F32)).astype(BF16)
        fresh = product(own, driven).astype(BF16)
        keep(fresh)
        if not last:
            results[1][...] = fresh

    if not side and not last:
        write_term(1 - slab, rest[0], results[0], results[2])


def squares_inputs(parts):
    pair = jnp.concatenate([part[...] for part in parts], axis=0)
    return (pair, times_i(pair, -1)), jnp.transpose(pair).astype(F32)


def own_sigma_kernel(pieces, scales, *rest):
    tops, lows = rest[pieces:]
    lefts, wide = squares_inputs(rest[:pieces])
    half = wide.shape[1] // 2
    upper = jnp.concatenate([left[:half] for left in lefts], axis=0)
    lower = jnp.concatenate([left[half:] for left in lefts], axis=0)
    for kind in range(2):
        weighted = (wide * scales[:, kind : kind + 1]).astype(BF16)
        tops[kind] = jnp.dot(upper, weighted, preferred_element_type=F32)
        lows[kind] = jnp.dot(lower, weighted[:, half:], preferred_element_type=F32)


def sigma_kernel(pieces, aliased, where, scales, tops, lows, *rest):
    lesser, greater, *token, held, sems = rest[pieces + aliased :]
    for ref in token:
        ref[...] = jnp.zeros_like(ref)
    lefts, wide = squares_inputs(rest[:pieces])
    half = wide.shape[1] // 2
    copies = []

    def send(kind, out, part, at):
        rows = slice(at * half, (at + 1) * half)
        copies.append(
            load(held.at[kind, part, rows], out.at[where[0], part, rows], sems.at[kind, 2 * part + at])
        )

    for kind, out in ((0, lesser), (1, greater)):
        weighted = (wide * scales[:, 2 + kind : 3 + kind]).astype(BF16)
        corners = []
        for part, left in enumerate(lefts):
            rows = slice(part * half, (part + 1) * half)
            top = jnp.dot(left[:half], weighted, preferred_element_type=F32) + tops[kind, rows]
            top = top.astype(BF16)
            held[kind, part, :half] = top
            send(kind, out, part, 0)
            corners.append(top[:, half:])
        for part, left in enumerate(lefts):
            rows = slice(part * half, (part + 1) * half)
            low = jnp.dot(left[half:], weighted[:, half:], preferred_element_type=F32)
            held[kind, part, half:, half:] = (low + lows[kind, rows]).astype(BF16)
            turned = jnp.transpose(corners[part])
            held[kind, part, half:, :half] = -turned if part else turned
            send(kind, out, part, 1)
    for copy in copies:
        copy.wait()


def whole(count):
    return [pl.BlockSpec(memory_space=pltpu.VMEM)] * count


SCALAR = pl.BlockSpec(memory_space=pltpu.SMEM)
FAR = pl.BlockSpec(memory_space=pltpu.HBM)
NEAR = pl.BlockSpec(memory_space=pltpu.VMEM)


def call(kernel, outs, specs, args, scratch=(), aliases=None):
    scalars, specs, args = (args[0], specs[1:], args[1:]) if specs[0] is SCALAR else ((), specs, args)
    count = len(scalars)
    aliases = {count - 1 + source: target for source, target in (aliases or {}).items()}

    def unpacked(*refs):
        if count:
            kernel([ref[0] for ref in refs[:count]], *refs[count:])
        else:
            kernel(*refs)

    specs, args = [SCALAR] * count + list(specs), (*scalars, *args)
    return pl.pallas_call(
        unpacked,
        out_shape=outs,
        in_specs=specs,
        out_specs=[NEAR] * len(outs),
        scratch_shapes=list(scratch),
        input_output_aliases=aliases,
        compiler_params=pltpu.CompilerParams(vmem_limit_bytes=24 * 2**20),
        cost_estimate=pl.CostEstimate(flops=1000, bytes_accessed=1000, transcendentals=0),
    )(*args)


def self_blocks(where, scales, own, other, blocks, previous):
    rows = sum(part.shape[0] for part in own)
    pieces = len(own)
    token = [] if previous else [jax.ShapeDtypeStruct((8, 128), F32)]
    sums = call(
        functools.partial(own_sigma_kernel, pieces),
        [
            jax.ShapeDtypeStruct((2, rows, rows), F32),
            jax.ShapeDtypeStruct((2, rows, rows // 2), F32),
        ],
        [NEAR] * (1 + pieces),
        (scales, *own),
    )
    return pl.pallas_call(
        functools.partial(sigma_kernel, pieces, len(previous)),
        out_shape=[jax.ShapeDtypeStruct(blocks, BF16)] * 2 + token,
        in_specs=[SCALAR] + [NEAR] * (3 + pieces) + [pl.BlockSpec(memory_space=pl.ANY)] * len(previous),
        out_specs=[pl.BlockSpec(memory_space=pl.ANY)] * 2 + [NEAR] * len(token),
        scratch_shapes=[
            pltpu.VMEM((2, 2, rows, rows), BF16),
            pltpu.SemaphoreType.DMA((2, 4)),
        ],
        input_output_aliases={4 + pieces + at: at for at in range(len(previous))},
        compiler_params=pltpu.CompilerParams(vmem_limit_bytes=24 * 2**20),
        cost_estimate=pl.CostEstimate(flops=1000, bytes_accessed=1000, transcendentals=0),
    )(where, scales, *sums, *other, *previous)


def body(energies, chips, precond, coupling, source, sigma_ret, occupation, shift_offsets, shift_weights):
    _, slabs, _, rows, modes = source.shape
    width = 2 * modes
    energy, chip = lax.axis_index("energy"), lax.axis_index("space")
    odd = lax.rem(chip, 2)
    inner = jnp.logical_and(chip > 0, chip < chips - 1).astype(jnp.int32)
    if LEAD_A:
        lead, valid = 1 - odd, [jnp.ones_like(inner), inner]
    else:
        lead, valid = odd, [inner, jnp.ones_like(inner)]
    where = [jnp.reshape(value, (1,)).astype(jnp.int32) for value in (lead, *valid, energy)]

    def at(e, c):
        return e * chips + c

    pairing_a, pairing_b = [], []
    for e in range(energies):
        for c in range(chips):
            pairing_a.append((at(e, c), at(e, c ^ 1)))
            if 0 < c < chips - 1:
                pairing_b.append((at(e, c), at(e, ((c + 1) ^ 1) - 1)))
            else:
                pairing_b.append((at(e, c), at(e ^ 1, c)))
    pairings = (pairing_a, pairing_b) if LEAD_A else (pairing_b, pairing_a)
    swap = [(at(e, c), at(e ^ 1, c)) for e in range(energies) for c in range(chips)]

    precond, source, sigma = precond[0], source[0], sigma_ret[0]
    pair = jax.ShapeDtypeStruct((rows, width), BF16)
    total = jax.ShapeDtypeStruct((rows, width), F32)
    matrix = jax.ShapeDtypeStruct((2, rows, rows), BF16)
    drive = jax.ShapeDtypeStruct((2, rows, modes), F32)
    states, arrived = [None, None], [None, None]
    owns, drives = [None, None], [None, None]

    precond, coupling, source = [
        pltpu.with_memory_space_constraint(array, pltpu.HBM) for array in (precond, coupling, source)
    ]
    states[0], send, owns[0], link, drives[0] = call(
        lead_kernel,
        [pair, pair, matrix, matrix, drive],
        [SCALAR, FAR, FAR, FAR],
        (where, precond, coupling, source),
        [pltpu.SemaphoreType.DMA((5,))],
    )
    arrived[0] = lax.ppermute(send, AXES, pairings[0])
    states[1], send, owns[1], within, drives[1], chain, term, link = call(
        trail_kernel,
        [pair, pair, matrix, matrix, drive, matrix, total, matrix],
        [SCALAR, FAR, FAR, FAR] + [NEAR] * 3,
        (where, precond, coupling, source, link, owns[0], states[0]),
        [pltpu.SemaphoreType.DMA((5,))],
        aliases={4: 7},
    )
    for sweep in range(1, SWEEPS):
        first, last = sweep == 1, sweep == SWEEPS - 1
        common = (where, within, link, sigma, *owns, *drives, *states, term)
        near = [SCALAR] + [NEAR] * 10
        *bases, send = call(
            functools.partial(base_kernel, "before", HELD[sweep], last),
            [total, total, total, pair],
            near + [NEAR],
            common + (send,),
        )
        arrived[1] = lax.ppermute(send, AXES, pairings[1])
        bases = call(
            functools.partial(base_kernel, "after", HELD[sweep], last),
            [total, total, total],
            near + [NEAR] * 3,
            common + tuple(bases),
            aliases={11: 0, 12: 1, 13: 2},
        )
        states, blocks, token = list(states), [], []
        for side in range(2):
            if last:
                pieces = 1 if side else LEAD_PIECES
                outs = [jax.ShapeDtypeStruct((rows // pieces, width), BF16)] * pieces
            else:
                outs = [pair, pair] if side else [pair, pair, total]
            if last:
                extra = token
            elif side:
                extra = [hand, bases[2]]
            else:
                extra = [within]
            results = call(
                functools.partial(step_kernel, side, last, len(outs)),
                outs,
                [SCALAR] + [NEAR] * (5 + len(extra)),
                (where, owns[side], chain, link, bases[side], arrived[side], *extra),
            )
            if last:
                others = [lax.ppermute(result, AXES, swap) for result in results]
                slab = (1 - lead if side else lead)[None].astype(jnp.int32)
                blocks = self_blocks(slab, scales, results, others, (slabs, 2, rows, rows), blocks)
                blocks, token = blocks[:2], blocks[2:]
                continue
            states[side], send = results[:2]
            if not side:
                arrived[0] = lax.ppermute(send, AXES, pairings[0])
                term = results[2]
                if first:
                    (hand,) = call(
                        hand_kernel, [matrix], [SCALAR, NEAR, NEAR], (where, chain, link)
                    )
                else:
                    (scales,) = call(
                        scales_kernel,
                        [jax.ShapeDtypeStruct((width, 8), F32)],
                        [SCALAR, NEAR, SCALAR, SCALAR],
                        (where, occupation, shift_offsets, shift_weights),
                    )
    return tuple(block[None] for block in blocks)


def solution(mesh):
    energies, chips = mesh.shape["energy"], mesh.shape["space"]
    placed = (
        P("energy", "space", None, None, None),
        P("space", None, None, None),
        P("energy", "space", None, None, None),
        P("energy", "space", None, None),
        P(),
        P(),
        P(),
    )
    return jax.shard_map(
        functools.partial(body, energies, chips),
        mesh=mesh,
        in_specs=placed,
        out_specs=(P("energy", "space", None, None, None), P("energy", "space", None, None, None)),
        check_vma=False,
    )
```

```python
import functools

import jax
import jax.numpy as jnp
from jax import lax
from jax.experimental import pallas as pl
from jax.experimental.pallas import tpu as pltpu
from jax.sharding import PartitionSpec as P

SWEEPS = 4
F32 = jnp.float32
BF16 = jnp.bfloat16
AXES = ("energy", "space")
LEAD_A = True
LEAD_PIECES = 2
HELD = {1: (0, 3), 2: (0, 3), 3: (2, 1)}


def times_i(pair, sign):
    half = pair.shape[1] // 2
    real, imag = pair[:, :half], pair[:, half:]
    if sign > 0:
        return jnp.concatenate([-imag, real], axis=1)
    return jnp.concatenate([imag, -real], axis=1)


def product(matrix, pair):
    out = jnp.dot(matrix[0], pair, preferred_element_type=F32)
    return out + jnp.dot(matrix[1], times_i(pair, 1), preferred_element_type=F32)


def transposed_dot(matrix, pair):
    return lax.dot_general(matrix, pair, (((0,), (0,)), ((), ())), preferred_element_type=F32)


def adjoint(matrix, pair):
    out = transposed_dot(matrix[0], pair)
    return out + transposed_dot(matrix[1], times_i(pair, -1))


def joined(ref, slab):
    return jnp.concatenate([ref[slab, 0], ref[slab, 1]], axis=1)


def load(source, held, sem):
    copy = pltpu.make_async_copy(source, held, sem)
    copy.start()
    return copy


def lead_kernel(where, precond, coupling, source, states, send, own, link, drive, sems):
    slab = where[0]
    copies = [
        load(source.at[slab], drive, sems.at[0]),
        load(precond.at[slab, 0], own.at[0], sems.at[1]),
        load(precond.at[slab, 1], own.at[1], sems.at[2]),
    ]
    links = [pltpu.make_async_copy(coupling.at[1, at], link.at[at], sems.at[3 + at]) for at in range(2)]

    @pl.when(slab == 1)
    def _():
        for copy in links:
            copy.start()

    copies[0].wait()
    pair = jnp.concatenate([drive[0], drive[1]], axis=1).astype(BF16)
    copies[1].wait()
    partial = jnp.dot(own[0], pair, preferred_element_type=F32)
    copies[2].wait()
    partial = partial + jnp.dot(own[1], times_i(pair, 1), preferred_element_type=F32)
    fresh = partial.astype(BF16)
    states[...] = fresh

    @pl.when(slab == 0)
    def _():
        send[...] = fresh

    @pl.when(slab == 1)
    def _():
        links[0].wait()
        handed = transposed_dot(link[0], fresh)
        links[1].wait()
        send[...] = (handed + transposed_dot(link[1], times_i(fresh, -1))).astype(BF16)


def trail_kernel(
    where, precond, coupling, source, given, lead, lead_states,
    states, send, own, inner, drive, chain, term, link, sems,
):
    slab = 1 - where[0]
    copies = [
        load(source.at[slab], drive, sems.at[0]),
        load(precond.at[slab, 0], own.at[0], sems.at[1]),
        load(precond.at[slab, 1], own.at[1], sems.at[2]),
    ]
    missing = pltpu.make_async_copy(coupling.at[1], link, sems.at[4])

    @pl.when(slab == 1)
    def _():
        missing.start()

    copies.append(load(coupling.at[0], inner, sems.at[3]))
    copies[0].wait()
    pair = jnp.concatenate([drive[0], drive[1]], axis=1).astype(BF16)
    copies[1].wait()
    partial = jnp.dot(own[0], pair, preferred_element_type=F32)
    copies[2].wait()
    partial = partial + jnp.dot(own[1], times_i(pair, 1), preferred_element_type=F32)
    fresh = partial.astype(BF16)
    states[...] = fresh

    @pl.when(slab == 1)
    def _():
        missing.wait()

    send_fresh(slab, link, fresh, send)

    def write_chain(matrix):
        both = product(matrix, jnp.concatenate([link[0], link[1]], axis=1))
        half = both.shape[1] // 2
        chain[0] = both[:, :half].astype(BF16)
        chain[1] = both[:, half:].astype(BF16)

    @pl.when(slab == 1)
    def _():
        write_chain(own)

    @pl.when(slab == 0)
    def _():
        write_chain(lead)

    copies[3].wait()
    write_term(slab, inner, lead_states, term)


def send_fresh(slab, link, fresh, send):
    @pl.when(slab == 1)
    def _():
        send[...] = adjoint(link, fresh).astype(BF16)

    @pl.when(slab == 0)
    def _():
        send[...] = fresh


def write_term(slab, inner, states, term):
    @pl.when(slab == 0)
    def _():
        term[...] = product(inner, states[...])

    @pl.when(slab == 1)
    def _():
        term[...] = adjoint(inner, states[...]).astype(BF16).astype(F32)


def hand_kernel(where, chain, link, hand):
    @pl.when(where[0] == 0)
    def _():
        both = adjoint(link, jnp.concatenate([chain[0], chain[1]], axis=1))
        half = both.shape[1] // 2
        hand[0] = both[:, :half].astype(BF16)
        hand[1] = both[:, half:].astype(BF16)


def base_kernel(
    kind, held, last, where, inner, link, sigma, own_a, own_b, source_a, source_b, states_a, states_b, term, *rest
):
    if kind == "before":
        base_a, base_b, base_send, send = rest[-4:]
        send[...] = rest[0][...]
    else:
        base_a, base_b, base_send = rest[-3:]
    parts = jnp.where(lax.rem(where[3], 2) == 0, held[0], held[1])
    here_a = jnp.logical_or(parts == 1, parts == 2)
    here_b = parts > 1
    if kind == "after":
        here_a, here_b = jnp.logical_not(here_a), jnp.logical_not(here_b)

    def local(slab, source, states):
        rows = states.shape[0]
        padded = jnp.concatenate([sigma[slab], jnp.zeros((6, rows), F32)], axis=0)
        columns = jnp.transpose(padded)
        real, imag = columns[:, 0:1], columns[:, 1:2]
        wide = states[...].astype(F32)
        half = wide.shape[1] // 2
        turned = jnp.concatenate([-wide[:, half:], wide[:, :half]], axis=1)
        drive = jnp.concatenate([source[0], source[1]], axis=1)
        return drive + (real * wide + imag * turned)

    @pl.when(jnp.logical_and(here_a, where[0] == 1))
    def _():
        handed = adjoint(inner, states_b[...]).astype(BF16).astype(F32)
        base_a[...] = product(own_a, (local(1, source_a, states_a) + handed).astype(BF16))

    @pl.when(jnp.logical_and(here_a, where[0] == 0))
    def _():
        base_a[...] = local(0, source_a, states_a) + product(inner, states_b[...])

    @pl.when(jnp.logical_and(here_b, where[0] == 1))
    def _():
        base_b[...] = local(0, source_b, states_b) + term[...]

    @pl.when(jnp.logical_and(here_b, where[0] == 0))
    def _():
        driven = (local(1, source_b, states_b) + term[...]).astype(BF16)
        solved = product(own_b, driven)
        base_b[...] = solved
        if not last:
            base_send[...] = adjoint(link, solved.astype(BF16))


def scales_kernel(where, occupation, offsets, weights, scales):
    energy = where[3]
    modes = occupation.shape[1]
    rows = []
    for at, target in ((0, energy), (1, 1 - energy)):
        total = jnp.float32(0)
        for shift in range(offsets.shape[1]):
            reached = energy + offsets[energy, shift] == target
            total = total + jnp.where(reached, weights[energy, shift], jnp.float32(0))
        weight = jnp.full((1, modes), total, F32) / modes
        filled = occupation[pl.ds(target, 1), :]
        for kind, share in ((0, filled), (1, 1.0 - filled)):
            row = weight * share
            rows.append(jnp.concatenate([row, row], axis=1))
    rows = jnp.concatenate(rows + [jnp.zeros((8 - len(rows), 2 * modes), F32)], axis=0)
    scales[...] = jnp.transpose(rows)


def step_kernel(side, last, outs, where, own, chain, link, base, arrived, *rest):
    results = rest[len(rest) - outs :]
    slab = 1 - where[0] if side else where[0]

    def message():
        return jnp.where(where[1 + side] != 0, arrived[...], jnp.zeros_like(arrived))

    def keep(fresh):
        if not last:
            results[0][...] = fresh
            return
        rows = fresh.shape[0] // outs
        for at, piece in enumerate(results):
            piece[...] = fresh[at * rows : (at + 1) * rows]

    @pl.when(slab == 1)
    def _():
        fresh = (base[...] + product(chain, message())).astype(BF16)
        keep(fresh)
        if side and not last:
            hand, base_send = rest[:2]
            results[1][...] = (base_send[...] + product(hand, message())).astype(BF16)
        elif not last:
            results[1][...] = adjoint(link, fresh).astype(BF16)

    @pl.when(slab == 0)
    def _():
        driven = (base[...] + message().astype(F32)).astype(BF16)
        fresh = product(own, driven).astype(BF16)
        keep(fresh)
        if not last:
            results[1][...] = fresh

    if not side and not last:
        write_term(1 - slab, rest[0], results[0], results[2])


def squares_inputs(parts):
    pair = jnp.concatenate([part[...] for part in parts], axis=0)
    return (pair, times_i(pair, -1)), jnp.transpose(pair).astype(F32)


def own_sigma_kernel(pieces, scales, *rest):
    tops, lows = rest[pieces:]
    lefts, wide = squares_inputs(rest[:pieces])
    half = wide.shape[1] // 2
    upper = jnp.concatenate([left[:half] for left in lefts], axis=0)
    lower = jnp.concatenate([left[half:] for left in lefts], axis=0)
    for kind in range(2):
        weighted = (wide * scales[:, kind : kind + 1]).astype(BF16)
        tops[kind] = jnp.dot(upper, weighted, preferred_element_type=F32)
        lows[kind] = jnp.dot(lower, weighted[:, half:], preferred_element_type=F32)


def sigma_kernel(pieces, aliased, where, scales, tops, lows, *rest):
    lesser, greater, *token, held, sems = rest[pieces + aliased :]
    for ref in token:
        ref[...] = jnp.zeros_like(ref)
    lefts, wide = squares_inputs(rest[:pieces])
    half = wide.shape[1] // 2
    copies = []

    def send(kind, out, part, at):
        rows = slice(at * half, (at + 1) * half)
        copies.append(
            load(held.at[kind, part, rows], out.at[where[0], part, rows], sems.at[kind, 2 * part + at])
        )

    for kind, out in ((0, lesser), (1, greater)):
        weighted = (wide * scales[:, 2 + kind : 3 + kind]).astype(BF16)
        corners = []
        for part, left in enumerate(lefts):
            rows = slice(part * half, (part + 1) * half)
            top = jnp.dot(left[:half], weighted, preferred_element_type=F32) + tops[kind, rows]
            top = top.astype(BF16)
            held[kind, part, :half] = top
            send(kind, out, part, 0)
            corners.append(top[:, half:])
        for part, left in enumerate(lefts):
            rows = slice(part * half, (part + 1) * half)
            low = jnp.dot(left[half:], weighted[:, half:], preferred_element_type=F32)
            held[kind, part, half:, half:] = (low + lows[kind, rows]).astype(BF16)
            turned = jnp.transpose(corners[part])
            held[kind, part, half:, :half] = -turned if part else turned
            send(kind, out, part, 1)
    for copy in copies:
        copy.wait()


def whole(count):
    return [pl.BlockSpec(memory_space=pltpu.VMEM)] * count


SCALAR = pl.BlockSpec(memory_space=pltpu.SMEM)
FAR = pl.BlockSpec(memory_space=pltpu.HBM)
NEAR = pl.BlockSpec(memory_space=pltpu.VMEM)


def call(kernel, outs, specs, args, scratch=(), aliases=None):
    scalars, specs, args = (args[0], specs[1:], args[1:]) if specs[0] is SCALAR else ((), specs, args)
    count = len(scalars)
    aliases = {count - 1 + source: target for source, target in (aliases or {}).items()}

    def unpacked(*refs):
        if count:
            kernel([ref[0] for ref in refs[:count]], *refs[count:])
        else:
            kernel(*refs)

    specs, args = [SCALAR] * count + list(specs), (*scalars, *args)
    return pl.pallas_call(
        unpacked,
        out_shape=outs,
        in_specs=specs,
        out_specs=[NEAR] * len(outs),
        scratch_shapes=list(scratch),
        input_output_aliases=aliases,
        compiler_params=pltpu.CompilerParams(vmem_limit_bytes=24 * 2**20),
        cost_estimate=pl.CostEstimate(flops=1000, bytes_accessed=1000, transcendentals=0),
    )(*args)


def self_blocks(where, scales, own, other, blocks, previous):
    rows = sum(part.shape[0] for part in own)
    pieces = len(own)
    token = [] if previous else [jax.ShapeDtypeStruct((8, 128), F32)]
    sums = call(
        functools.partial(own_sigma_kernel, pieces),
        [
            jax.ShapeDtypeStruct((2, rows, rows), F32),
            jax.ShapeDtypeStruct((2, rows, rows // 2), F32),
        ],
        [NEAR] * (1 + pieces),
        (scales, *own),
    )
    return pl.pallas_call(
        functools.partial(sigma_kernel, pieces, len(previous)),
        out_shape=[jax.ShapeDtypeStruct(blocks, BF16)] * 2 + token,
        in_specs=[SCALAR] + [NEAR] * (3 + pieces) + [pl.BlockSpec(memory_space=pl.ANY)] * len(previous),
        out_specs=[pl.BlockSpec(memory_space=pl.ANY)] * 2 + [NEAR] * len(token),
        scratch_shapes=[
            pltpu.VMEM((2, 2, rows, rows), BF16),
            pltpu.SemaphoreType.DMA((2, 4)),
        ],
        input_output_aliases={4 + pieces + at: at for at in range(len(previous))},
        compiler_params=pltpu.CompilerParams(vmem_limit_bytes=24 * 2**20),
        cost_estimate=pl.CostEstimate(flops=1000, bytes_accessed=1000, transcendentals=0),
    )(where, scales, *sums, *other, *previous)


def body(energies, chips, precond, coupling, source, sigma_ret, occupation, shift_offsets, shift_weights):
    _, slabs, _, rows, modes = source.shape
    width = 2 * modes
    energy, chip = lax.axis_index("energy"), lax.axis_index("space")
    odd = lax.rem(chip, 2)
    inner = jnp.logical_and(chip > 0, chip < chips - 1).astype(jnp.int32)
    if LEAD_A:
        lead, valid = 1 - odd, [jnp.ones_like(inner), inner]
    else:
        lead, valid = odd, [inner, jnp.ones_like(inner)]
    where = [jnp.reshape(value, (1,)).astype(jnp.int32) for value in (lead, *valid, energy)]

    def at(e, c):
        return e * chips + c

    pairing_a, pairing_b = [], []
    for e in range(energies):
        for c in range(chips):
            pairing_a.append((at(e, c), at(e, c ^ 1)))
            if 0 < c < chips - 1:
                pairing_b.append((at(e, c), at(e, ((c + 1) ^ 1) - 1)))
            else:
                pairing_b.append((at(e, c), at(e ^ 1, c)))
    pairings = (pairing_a, pairing_b) if LEAD_A else (pairing_b, pairing_a)
    swap = [(at(e, c), at(e ^ 1, c)) for e in range(energies) for c in range(chips)]

    precond, source, sigma = precond[0], source[0], sigma_ret[0]
    pair = jax.ShapeDtypeStruct((rows, width), BF16)
    total = jax.ShapeDtypeStruct((rows, width), F32)
    matrix = jax.ShapeDtypeStruct((2, rows, rows), BF16)
    drive = jax.ShapeDtypeStruct((2, rows, modes), F32)
    states, arrived = [None, None], [None, None]
    owns, drives = [None, None], [None, None]

    precond, coupling, source = [
        pltpu.with_memory_space_constraint(array, pltpu.HBM) for array in (precond, coupling, source)
    ]
    states[0], send, owns[0], link, drives[0] = call(
        lead_kernel,
        [pair, pair, matrix, matrix, drive],
        [SCALAR, FAR, FAR, FAR],
        (where, precond, coupling, source),
        [pltpu.SemaphoreType.DMA((5,))],
    )
    arrived[0] = lax.ppermute(send, AXES, pairings[0])
    states[1], send, owns[1], within, drives[1], chain, term, link = call(
        trail_kernel,
        [pair, pair, matrix, matrix, drive, matrix, total, matrix],
        [SCALAR, FAR, FAR, FAR] + [NEAR] * 3,
        (where, precond, coupling, source, link, owns[0], states[0]),
        [pltpu.SemaphoreType.DMA((5,))],
        aliases={4: 7},
    )
    for sweep in range(1, SWEEPS):
        first, last = sweep == 1, sweep == SWEEPS - 1
        common = (where, within, link, sigma, *owns, *drives, *states, term)
        near = [SCALAR] + [NEAR] * 10
        *bases, send = call(
            functools.partial(base_kernel, "before", HELD[sweep], last),
            [total, total, total, pair],
            near + [NEAR],
            common + (send,),
        )
        arrived[1] = lax.ppermute(send, AXES, pairings[1])
        bases = call(
            functools.partial(base_kernel, "after", HELD[sweep], last),
            [total, total, total],
            near + [NEAR] * 3,
            common + tuple(bases),
            aliases={11: 0, 12: 1, 13: 2},
        )
        states, blocks, token = list(states), [], []
        for side in range(2):
            if last:
                pieces = 1 if side else LEAD_PIECES
                outs = [jax.ShapeDtypeStruct((rows // pieces, width), BF16)] * pieces
            else:
                outs = [pair, pair] if side else [pair, pair, total]
            if last:
                extra = token
            elif side:
                extra = [hand, bases[2]]
            else:
                extra = [within]
            results = call(
                functools.partial(step_kernel, side, last, len(outs)),
                outs,
                [SCALAR] + [NEAR] * (5 + len(extra)),
                (where, owns[side], chain, link, bases[side], arrived[side], *extra),
            )
            if last:
                others = [lax.ppermute(result, AXES, swap) for result in results]
                slab = (1 - lead if side else lead)[None].astype(jnp.int32)
                blocks = self_blocks(slab, scales, results, others, (slabs, 2, rows, rows), blocks)
                blocks, token = blocks[:2], blocks[2:]
                continue
            states[side], send = results[:2]
            if not side:
                arrived[0] = lax.ppermute(send, AXES, pairings[0])
                term = results[2]
                if first:
                    (hand,) = call(
                        hand_kernel, [matrix], [SCALAR, NEAR, NEAR], (where, chain, link)
                    )
                else:
                    (scales,) = call(
                        scales_kernel,
                        [jax.ShapeDtypeStruct((width, 8), F32)],
                        [SCALAR, NEAR, SCALAR, SCALAR],
                        (where, occupation, shift_offsets, shift_weights),
                    )
    return tuple(block[None] for block in blocks)


def solution(mesh):
    energies, chips = mesh.shape["energy"], mesh.shape["space"]
    placed = (
        P("energy", "space", None, None, None),
        P("space", None, None, None),
        P("energy", "space", None, None, None),
        P("energy", "space", None, None),
        P(),
        P(),
        P(),
    )
    return jax.shard_map(
        functools.partial(body, energies, chips),
        mesh=mesh,
        in_specs=placed,
        out_specs=(P("energy", "space", None, None, None), P("energy", "space", None, None, None)),
        check_vma=False,
    )
```

```python
import functools

import jax
import jax.numpy as jnp
from jax import lax
from jax.experimental import pallas as pl
from jax.experimental.pallas import tpu as pltpu
from jax.sharding import PartitionSpec as P

SWEEPS = 4
F32 = jnp.float32
BF16 = jnp.bfloat16
AXES = ("energy", "space")
LEAD_A = True
LEAD_PIECES = 2
HELD = {1: (0, 3), 2: (0, 3), 3: (2, 1)}


def times_i(pair, sign):
    half = pair.shape[1] // 2
    real, imag = pair[:, :half], pair[:, half:]
    if sign > 0:
        return jnp.concatenate([-imag, real], axis=1)
    return jnp.concatenate([imag, -real], axis=1)


def product(matrix, pair):
    out = jnp.dot(matrix[0], pair, preferred_element_type=F32)
    return out + jnp.dot(matrix[1], times_i(pair, 1), preferred_element_type=F32)


def transposed_dot(matrix, pair):
    return lax.dot_general(matrix, pair, (((0,), (0,)), ((), ())), preferred_element_type=F32)


def adjoint(matrix, pair):
    out = transposed_dot(matrix[0], pair)
    return out + transposed_dot(matrix[1], times_i(pair, -1))


def joined(ref, slab):
    return jnp.concatenate([ref[slab, 0], ref[slab, 1]], axis=1)


def load(source, held, sem):
    copy = pltpu.make_async_copy(source, held, sem)
    copy.start()
    return copy


def lead_kernel(where, precond, coupling, source, states, send, own, link, drive, sems):
    slab = where[0]
    copies = [
        load(source.at[slab], drive, sems.at[0]),
        load(precond.at[slab, 0], own.at[0], sems.at[1]),
        load(precond.at[slab, 1], own.at[1], sems.at[2]),
    ]
    links = [pltpu.make_async_copy(coupling.at[1, at], link.at[at], sems.at[3 + at]) for at in range(2)]

    @pl.when(slab == 1)
    def _():
        for copy in links:
            copy.start()

    copies[0].wait()
    pair = jnp.concatenate([drive[0], drive[1]], axis=1).astype(BF16)
    copies[1].wait()
    partial = jnp.dot(own[0], pair, preferred_element_type=F32)
    copies[2].wait()
    partial = partial + jnp.dot(own[1], times_i(pair, 1), preferred_element_type=F32)
    fresh = partial.astype(BF16)
    states[...] = fresh

    @pl.when(slab == 0)
    def _():
        send[...] = fresh

    @pl.when(slab == 1)
    def _():
        links[0].wait()
        handed = transposed_dot(link[0], fresh)
        links[1].wait()
        send[...] = (handed + transposed_dot(link[1], times_i(fresh, -1))).astype(BF16)


def trail_kernel(
    where, precond, coupling, source, given, lead, lead_states,
    states, send, own, inner, drive, chain, term, link, sems,
):
    slab = 1 - where[0]
    copies = [
        load(source.at[slab], drive, sems.at[0]),
        load(precond.at[slab, 0], own.at[0], sems.at[1]),
        load(precond.at[slab, 1], own.at[1], sems.at[2]),
    ]
    missing = pltpu.make_async_copy(coupling.at[1], link, sems.at[4])

    @pl.when(slab == 1)
    def _():
        missing.start()

    copies.append(load(coupling.at[0], inner, sems.at[3]))
    copies[0].wait()
    pair = jnp.concatenate([drive[0], drive[1]], axis=1).astype(BF16)
    copies[1].wait()
    partial = jnp.dot(own[0], pair, preferred_element_type=F32)
    copies[2].wait()
    partial = partial + jnp.dot(own[1], times_i(pair, 1), preferred_element_type=F32)
    fresh = partial.astype(BF16)
    states[...] = fresh

    @pl.when(slab == 1)
    def _():
        missing.wait()

    send_fresh(slab, link, fresh, send)

    def write_chain(matrix):
        both = product(matrix, jnp.concatenate([link[0], link[1]], axis=1))
        half = both.shape[1] // 2
        chain[0] = both[:, :half].astype(BF16)
        chain[1] = both[:, half:].astype(BF16)

    @pl.when(slab == 1)
    def _():
        write_chain(own)

    @pl.when(slab == 0)
    def _():
        write_chain(lead)

    copies[3].wait()
    write_term(slab, inner, lead_states, term)


def send_fresh(slab, link, fresh, send):
    @pl.when(slab == 1)
    def _():
        send[...] = adjoint(link, fresh).astype(BF16)

    @pl.when(slab == 0)
    def _():
        send[...] = fresh


def write_term(slab, inner, states, term):
    @pl.when(slab == 0)
    def _():
        term[...] = product(inner, states[...])

    @pl.when(slab == 1)
    def _():
        term[...] = adjoint(inner, states[...]).astype(BF16).astype(F32)


def hand_kernel(where, chain, link, hand):
    @pl.when(where[0] == 0)
    def _():
        both = adjoint(link, jnp.concatenate([chain[0], chain[1]], axis=1))
        half = both.shape[1] // 2
        hand[0] = both[:, :half].astype(BF16)
        hand[1] = both[:, half:].astype(BF16)


def base_kernel(
    kind, held, last, where, inner, link, sigma, own_a, own_b, source_a, source_b, states_a, states_b, term, *rest
):
    if kind == "before":
        base_a, base_b, base_send, send = rest[-4:]
        send[...] = rest[0][...]
    else:
        base_a, base_b, base_send = rest[-3:]
    parts = jnp.where(lax.rem(where[3], 2) == 0, held[0], held[1])
    here_a = jnp.logical_or(parts == 1, parts == 2)
    here_b = parts > 1
    if kind == "after":
        here_a, here_b = jnp.logical_not(here_a), jnp.logical_not(here_b)

    def local(slab, source, states):
        rows = states.shape[0]
        padded = jnp.concatenate([sigma[slab], jnp.zeros((6, rows), F32)], axis=0)
        columns = jnp.transpose(padded)
        real, imag = columns[:, 0:1], columns[:, 1:2]
        wide = states[...].astype(F32)
        half = wide.shape[1] // 2
        turned = jnp.concatenate([-wide[:, half:], wide[:, :half]], axis=1)
        drive = jnp.concatenate([source[0], source[1]], axis=1)
        return drive + (real * wide + imag * turned)

    @pl.when(jnp.logical_and(here_a, where[0] == 1))
    def _():
        handed = adjoint(inner, states_b[...]).astype(BF16).astype(F32)
        base_a[...] = product(own_a, (local(1, source_a, states_a) + handed).astype(BF16))

    @pl.when(jnp.logical_and(here_a, where[0] == 0))
    def _():
        base_a[...] = local(0, source_a, states_a) + product(inner, states_b[...])

    @pl.when(jnp.logical_and(here_b, where[0] == 1))
    def _():
        base_b[...] = local(0, source_b, states_b) + term[...]

    @pl.when(jnp.logical_and(here_b, where[0] == 0))
    def _():
        driven = (local(1, source_b, states_b) + term[...]).astype(BF16)
        solved = product(own_b, driven)
        base_b[...] = solved
        if not last:
            base_send[...] = adjoint(link, solved.astype(BF16))


def scales_kernel(where, occupation, offsets, weights, scales):
    energy = where[3]
    modes = occupation.shape[1]
    rows = []
    for at, target in ((0, energy), (1, 1 - energy)):
        total = jnp.float32(0)
        for shift in range(offsets.shape[1]):
            reached = energy + offsets[energy, shift] == target
            total = total + jnp.where(reached, weights[energy, shift], jnp.float32(0))
        weight = jnp.full((1, modes), total, F32) / modes
        filled = occupation[pl.ds(target, 1), :]
        for kind, share in ((0, filled), (1, 1.0 - filled)):
            row = weight * share
            rows.append(jnp.concatenate([row, row], axis=1))
    rows = jnp.concatenate(rows + [jnp.zeros((8 - len(rows), 2 * modes), F32)], axis=0)
    scales[...] = jnp.transpose(rows)


def step_kernel(side, last, outs, where, own, chain, link, base, arrived, *rest):
    results = rest[len(rest) - outs :]
    slab = 1 - where[0] if side else where[0]

    def message():
        if (side == 0) == LEAD_A:
            return arrived[...]
        return jnp.where(where[1 + side] != 0, arrived[...], jnp.zeros_like(arrived))

    def keep(fresh):
        if not last:
            results[0][...] = fresh
            return
        rows = fresh.shape[0] // outs
        for at, piece in enumerate(results):
            piece[...] = fresh[at * rows : (at + 1) * rows]

    @pl.when(slab == 1)
    def _():
        fresh = (base[...] + product(chain, message())).astype(BF16)
        keep(fresh)
        if side and not last:
            hand, base_send = rest[:2]
            results[1][...] = (base_send[...] + product(hand, message())).astype(BF16)
        elif not last:
            results[1][...] = adjoint(link, fresh).astype(BF16)

    @pl.when(slab == 0)
    def _():
        driven = (base[...] + message().astype(F32)).astype(BF16)
        fresh = product(own, driven).astype(BF16)
        keep(fresh)
        if not last:
            results[1][...] = fresh

    if not side and not last:
        write_term(1 - slab, rest[0], results[0], results[2])


def squares_inputs(parts):
    pair = jnp.concatenate([part[...] for part in parts], axis=0)
    return (pair, times_i(pair, -1)), jnp.transpose(pair).astype(F32)


def own_sigma_kernel(pieces, scales, *rest):
    tops, lows = rest[pieces:]
    lefts, wide = squares_inputs(rest[:pieces])
    half = wide.shape[1] // 2
    upper = jnp.concatenate([left[:half] for left in lefts], axis=0)
    lower = jnp.concatenate([left[half:] for left in lefts], axis=0)
    for kind in range(2):
        weighted = (wide * scales[:, kind : kind + 1]).astype(BF16)
        tops[kind] = jnp.dot(upper, weighted, preferred_element_type=F32)
        lows[kind] = jnp.dot(lower, weighted[:, half:], preferred_element_type=F32)


def sigma_kernel(pieces, aliased, where, scales, tops, lows, *rest):
    lesser, greater, *token, held, sems = rest[pieces + aliased :]
    for ref in token:
        ref[...] = jnp.zeros_like(ref)
    lefts, wide = squares_inputs(rest[:pieces])
    half = wide.shape[1] // 2
    copies = []

    def send(kind, out, part, at):
        rows = slice(at * half, (at + 1) * half)
        copies.append(
            load(held.at[kind, part, rows], out.at[where[0], part, rows], sems.at[kind, 2 * part + at])
        )

    for kind, out in ((0, lesser), (1, greater)):
        weighted = (wide * scales[:, 2 + kind : 3 + kind]).astype(BF16)
        corners = []
        for part, left in enumerate(lefts):
            rows = slice(part * half, (part + 1) * half)
            top = jnp.dot(left[:half], weighted, preferred_element_type=F32) + tops[kind, rows]
            top = top.astype(BF16)
            held[kind, part, :half] = top
            send(kind, out, part, 0)
            corners.append(top[:, half:])
        for part, left in enumerate(lefts):
            rows = slice(part * half, (part + 1) * half)
            low = jnp.dot(left[half:], weighted[:, half:], preferred_element_type=F32)
            held[kind, part, half:, half:] = (low + lows[kind, rows]).astype(BF16)
            turned = jnp.transpose(corners[part])
            held[kind, part, half:, :half] = -turned if part else turned
            send(kind, out, part, 1)
    for copy in copies:
        copy.wait()


def whole(count):
    return [pl.BlockSpec(memory_space=pltpu.VMEM)] * count


SCALAR = pl.BlockSpec(memory_space=pltpu.SMEM)
FAR = pl.BlockSpec(memory_space=pltpu.HBM)
NEAR = pl.BlockSpec(memory_space=pltpu.VMEM)


def call(kernel, outs, specs, args, scratch=(), aliases=None):
    scalars, specs, args = (args[0], specs[1:], args[1:]) if specs[0] is SCALAR else ((), specs, args)
    count = len(scalars)
    aliases = {count - 1 + source: target for source, target in (aliases or {}).items()}

    def unpacked(*refs):
        if count:
            kernel([ref[0] for ref in refs[:count]], *refs[count:])
        else:
            kernel(*refs)

    specs, args = [SCALAR] * count + list(specs), (*scalars, *args)
    return pl.pallas_call(
        unpacked,
        out_shape=outs,
        in_specs=specs,
        out_specs=[NEAR] * len(outs),
        scratch_shapes=list(scratch),
        input_output_aliases=aliases,
        compiler_params=pltpu.CompilerParams(vmem_limit_bytes=24 * 2**20),
        cost_estimate=pl.CostEstimate(flops=1000, bytes_accessed=1000, transcendentals=0),
    )(*args)


def self_blocks(where, scales, own, other, blocks, previous):
    rows = sum(part.shape[0] for part in own)
    pieces = len(own)
    token = [] if previous else [jax.ShapeDtypeStruct((8, 128), F32)]
    sums = call(
        functools.partial(own_sigma_kernel, pieces),
        [
            jax.ShapeDtypeStruct((2, rows, rows), F32),
            jax.ShapeDtypeStruct((2, rows, rows // 2), F32),
        ],
        [NEAR] * (1 + pieces),
        (scales, *own),
    )
    return pl.pallas_call(
        functools.partial(sigma_kernel, pieces, len(previous)),
        out_shape=[jax.ShapeDtypeStruct(blocks, BF16)] * 2 + token,
        in_specs=[SCALAR] + [NEAR] * (3 + pieces) + [pl.BlockSpec(memory_space=pl.ANY)] * len(previous),
        out_specs=[pl.BlockSpec(memory_space=pl.ANY)] * 2 + [NEAR] * len(token),
        scratch_shapes=[
            pltpu.VMEM((2, 2, rows, rows), BF16),
            pltpu.SemaphoreType.DMA((2, 4)),
        ],
        input_output_aliases={4 + pieces + at: at for at in range(len(previous))},
        compiler_params=pltpu.CompilerParams(vmem_limit_bytes=24 * 2**20),
        cost_estimate=pl.CostEstimate(flops=1000, bytes_accessed=1000, transcendentals=0),
    )(where, scales, *sums, *other, *previous)


def body(energies, chips, precond, coupling, source, sigma_ret, occupation, shift_offsets, shift_weights):
    _, slabs, _, rows, modes = source.shape
    width = 2 * modes
    energy, chip = lax.axis_index("energy"), lax.axis_index("space")
    odd = lax.rem(chip, 2)
    inner = jnp.logical_and(chip > 0, chip < chips - 1).astype(jnp.int32)
    if LEAD_A:
        lead, valid = 1 - odd, [jnp.ones_like(inner), inner]
    else:
        lead, valid = odd, [inner, jnp.ones_like(inner)]
    where = [jnp.reshape(value, (1,)).astype(jnp.int32) for value in (lead, *valid, energy)]

    def at(e, c):
        return e * chips + c

    pairing_a, pairing_b = [], []
    for e in range(energies):
        for c in range(chips):
            pairing_a.append((at(e, c), at(e, c ^ 1)))
            if 0 < c < chips - 1:
                pairing_b.append((at(e, c), at(e, ((c + 1) ^ 1) - 1)))
            else:
                pairing_b.append((at(e, c), at(e ^ 1, c)))
    pairings = (pairing_a, pairing_b) if LEAD_A else (pairing_b, pairing_a)
    swap = [(at(e, c), at(e ^ 1, c)) for e in range(energies) for c in range(chips)]

    precond, source, sigma = precond[0], source[0], sigma_ret[0]
    pair = jax.ShapeDtypeStruct((rows, width), BF16)
    total = jax.ShapeDtypeStruct((rows, width), F32)
    matrix = jax.ShapeDtypeStruct((2, rows, rows), BF16)
    drive = jax.ShapeDtypeStruct((2, rows, modes), F32)
    states, arrived = [None, None], [None, None]
    owns, drives = [None, None], [None, None]

    precond, coupling, source = [
        pltpu.with_memory_space_constraint(array, pltpu.HBM) for array in (precond, coupling, source)
    ]
    states[0], send, owns[0], link, drives[0] = call(
        lead_kernel,
        [pair, pair, matrix, matrix, drive],
        [SCALAR, FAR, FAR, FAR],
        (where, precond, coupling, source),
        [pltpu.SemaphoreType.DMA((5,))],
    )
    arrived[0] = lax.ppermute(send, AXES, pairings[0])
    states[1], send, owns[1], within, drives[1], chain, term, link = call(
        trail_kernel,
        [pair, pair, matrix, matrix, drive, matrix, total, matrix],
        [SCALAR, FAR, FAR, FAR] + [NEAR] * 3,
        (where, precond, coupling, source, link, owns[0], states[0]),
        [pltpu.SemaphoreType.DMA((5,))],
        aliases={4: 7},
    )
    for sweep in range(1, SWEEPS):
        first, last = sweep == 1, sweep == SWEEPS - 1
        common = (where, within, link, sigma, *owns, *drives, *states, term)
        near = [SCALAR] + [NEAR] * 10
        *bases, send = call(
            functools.partial(base_kernel, "before", HELD[sweep], last),
            [total, total, total, pair],
            near + [NEAR],
            common + (send,),
        )
        arrived[1] = lax.ppermute(send, AXES, pairings[1])
        bases = call(
            functools.partial(base_kernel, "after", HELD[sweep], last),
            [total, total, total],
            near + [NEAR] * 3,
            common + tuple(bases),
            aliases={11: 0, 12: 1, 13: 2},
        )
        states, blocks, token = list(states), [], []
        for side in range(2):
            if last:
                pieces = 1 if side else LEAD_PIECES
                outs = [jax.ShapeDtypeStruct((rows // pieces, width), BF16)] * pieces
            else:
                outs = [pair, pair] if side else [pair, pair, total]
            if last:
                extra = token
            elif side:
                extra = [hand, bases[2]]
            else:
                extra = [within]
            results = call(
                functools.partial(step_kernel, side, last, len(outs)),
                outs,
                [SCALAR] + [NEAR] * (5 + len(extra)),
                (where, owns[side], chain, link, bases[side], arrived[side], *extra),
            )
            if last:
                others = [lax.ppermute(result, AXES, swap) for result in results]
                slab = (1 - lead if side else lead)[None].astype(jnp.int32)
                blocks = self_blocks(slab, scales, results, others, (slabs, 2, rows, rows), blocks)
                blocks, token = blocks[:2], blocks[2:]
                continue
            states[side], send = results[:2]
            if not side:
                arrived[0] = lax.ppermute(send, AXES, pairings[0])
                term = results[2]
                if first:
                    (hand,) = call(
                        hand_kernel, [matrix], [SCALAR, NEAR, NEAR], (where, chain, link)
                    )
                else:
                    (scales,) = call(
                        scales_kernel,
                        [jax.ShapeDtypeStruct((width, 8), F32)],
                        [SCALAR, NEAR, SCALAR, SCALAR],
                        (where, occupation, shift_offsets, shift_weights),
                    )
    return tuple(block[None] for block in blocks)


def solution(mesh):
    energies, chips = mesh.shape["energy"], mesh.shape["space"]
    placed = (
        P("energy", "space", None, None, None),
        P("space", None, None, None),
        P("energy", "space", None, None, None),
        P("energy", "space", None, None),
        P(),
        P(),
        P(),
    )
    return jax.shard_map(
        functools.partial(body, energies, chips),
        mesh=mesh,
        in_specs=placed,
        out_specs=(P("energy", "space", None, None, None), P("energy", "space", None, None, None)),
        check_vma=False,
    )
```
